32 devices in a mesh: grp: 2 (over y), vec: 4 (over z), wlk: 4 (over x, core).
Axes of the slice: x: 2, y: 2, z: 4, core: 2. Of those that a mesh axis runs over, the one named last changes fastest.
Arguments:
- cholesky: bfloat16 [48, 64, 512], P(('grp', 'vec')), parts along dimension 0
- orbitals: float32 [32, 64, 512], P(('grp', 'vec', 'wlk')), parts along dimension 0, may hold values from -6 to 6
- log_weights: float32 [32], P(('grp', 'vec', 'wlk')), parts along dimension 0, may hold values from -6 to 6
- parents: int32 [32], P(('grp', 'vec', 'wlk')), parts along dimension 0, may hold values from 0 to 3
- propagator: float32 [1024, 512], P('grp'), parts along dimension 0
Outputs:
- new_orbitals: float32 [32, 64, 512], P(('grp', 'vec', 'wlk')), parts along dimension 0
- new_log_weights: float32 [32], P(('grp', 'vec', 'wlk')), parts along dimension 0
The draws below stay inside these ranges and needn't reach their ends.
There are 2 independent parts, one for each index of `grp`. The reference program is written for one: setup_inputs(seed, part) draws one part's arguments, and reference() takes and returns one part's arrays. A program takes and returns all parts, laid end to end along the dimension named above; each array names one. Nothing has to cross between parts.
Inputs may be any that keep to these rules, and one draw needn't show every extreme that they name: parents[w] counts within the aligned block of 4 consecutive walkers that holds w.
All inputs are finite; a program needn't handle non-finite values.
Results may differ from the reference program's by a relative error of at most 0.02.
Values may be sent and summed in bfloat16 or wider, within the bound.
No kernel may reach another device: no remote copies, remote signals or barrier semaphores. Data moves between devices by JAX's collectives and lax.ppermute only.
A program may use at most 64 MiB of HBM per device.

```python
import math
import jax
import jax.numpy as jnp
import numpy as np
from jax import lax

NORB = 512
NOCC = 64
NS_ITERS = 2
NCHOL = 24
POPULATION = 4
WALKERS = 16


def draw_cholesky(key, part):
    noise_key = jax.random.fold_in(key, 11)
    position = jnp.arange(NCHOL, dtype=jnp.float32) / max(NCHOL - 1, 1)
    samples = jax.random.normal(noise_key, (NCHOL, NOCC, NORB), jnp.float32)
    falloff = 3.0 ** (1.0 - position)
    return (samples * falloff[:, None, None] / math.sqrt(NORB)).astype(jnp.bfloat16)


def draw_orbitals(key, part):
    noise_key = jax.random.fold_in(key, 37)
    values = jnp.clip(jax.random.normal(noise_key, (WALKERS, NOCC, NORB), jnp.float32), -6.0, 6.0)
    return values.astype(jnp.float32)


def draw_propagator(key, part):
    noise_key = jax.random.fold_in(key, 23)
    samples = jax.random.normal(noise_key, (NORB, NORB), jnp.float32)
    return jnp.eye(NORB, dtype=jnp.float32) + 0.5 * samples / math.sqrt(NORB)


def set_ends(result, stream_key, least, top_value):
    place = [jax.random.randint(jax.random.fold_in(stream_key, axis), (), 0, length) for axis, length in enumerate(result.shape)]
    main_axis = result.shape.index(max(result.shape))
    beside = place[:main_axis] + [(place[main_axis] + 1) % result.shape[main_axis]] + place[main_axis + 1:]
    return result.at[tuple(place)].set(least).at[tuple(beside)].set(top_value)


def block_scale(own_key, extent, shards, smallest, top_value):
    level = 1.0
    for dim, parts in shards:
        steps = jax.random.uniform(jax.random.fold_in(jax.random.fold_in(own_key, 6), dim), (parts,), jnp.float32, smallest / len(shards), top_value / len(shards))
        level = level * jnp.repeat(jnp.exp(steps), extent[dim] // parts).reshape((-1,) + (1,) * (len(extent) - 1 - dim))
    return level


def cumulative_ranks(count, lean):
    weights = [(1 << 20) // math.isqrt(standing ** lean) + 1 for standing in range(1, count + 1)]
    deviation = 1 + sum(weights) // (1 << 30)
    return np.cumsum(np.array([max(1, weight // deviation) for weight in weights]))


def ranked(key, shape, number_of, slope):
    table = cumulative_ranks(number_of, slope)
    ticket = jax.random.randint(jax.random.fold_in(key, 1), shape, 0, int(table[number_of - 1]))
    rank = jnp.searchsorted(jnp.asarray(table, jnp.int32), ticket, side="right")
    return jax.random.permutation(jax.random.fold_in(key, 2), number_of)[rank].astype(jnp.int32)


def gaussian(stream_key, dims, scale, limit, cuts=(), held_as=jnp.bfloat16):
    loudness = block_scale(stream_key, dims, cuts, -0.22, 0.18) if cuts else 1.0
    result = jax.random.normal(stream_key, dims, jnp.float32) * scale * loudness
    return jnp.minimum(jnp.maximum(result, -limit), limit).astype(held_as)


def setup_inputs(seed: int = 0, part: int = 0) -> dict:
    key_list = jax.random.split(jax.random.key(seed), 6)
    part_splits = jax.random.split(jax.random.fold_in(key_list[5], part), 6)
    return {
        "cholesky": draw_cholesky(jax.random.fold_in(jax.random.fold_in(key_list[5], part), 71), part),
        "orbitals": draw_orbitals(jax.random.fold_in(jax.random.fold_in(key_list[5], part), 71), part),
        "log_weights": gaussian(part_splits[2], (WALKERS,), 1.0, 6.0, ((0, 16),), jnp.float32),
        "parents": set_ends(ranked(part_splits[3], (WALKERS,), POPULATION, 2), jax.random.fold_in(part_splits[3], 3), 0, POPULATION - 1).astype(jnp.int32),
        "propagator": draw_propagator(jax.random.fold_in(jax.random.fold_in(key_list[5], part), 71), part),
    }


gradient_step = 0.25
energy_step = 0.002
epsilon = 1e-06

def reference(cholesky, orbitals, log_weights, parents, propagator):
    norm_scale = 1.0 / math.sqrt(NCHOL)
    chol_flat = cholesky.astype(jnp.float32).reshape(NCHOL * NOCC, NORB)
    identity = jnp.eye(NOCC, dtype=jnp.float32)

    def per_walker(orbital_rows):
        rounded = orbital_rows.astype(jnp.bfloat16)
        rounded = lax.optimization_barrier(rounded)
        theta = rounded.astype(jnp.float32)
        product = jnp.dot(theta, chol_flat.T)
        product = lax.optimization_barrier(product.astype(jnp.bfloat16))
        blocks = product.astype(jnp.float32).reshape(NOCC, NCHOL, NOCC)
        traces = lax.optimization_barrier(jnp.sum(blocks * identity[:, None, :], axis=(0, 2)))
        swapped = jnp.transpose(blocks, (2, 1, 0))
        exchange_sum = lax.optimization_barrier(jnp.sum(blocks * swapped, axis=(0, 2)))
        energy = 0.5 * norm_scale * jnp.sum(traces * traces - exchange_sum)
        adjoint = norm_scale * (traces[None, :, None] * identity[:, None, :] - swapped)
        adjoint = lax.optimization_barrier(adjoint.astype(jnp.bfloat16))
        adjoint = adjoint.astype(jnp.float32).reshape(NOCC, NCHOL * NOCC)
        gradient = jnp.dot(adjoint, chol_flat)
        return (energy, gradient)
    energies, gradients = lax.map(per_walker, orbitals)
    stepped = orbitals - gradient_step * gradients
    shifted = log_weights - energy_step * energies
    walker_ids = jnp.arange(WALKERS, dtype=jnp.int32)
    source = walker_ids // POPULATION * POPULATION + parents.astype(jnp.int32)
    chosen = stepped[source]
    new_log_weights = shifted[source]
    propagated = jnp.einsum('wjq,pq->wjp', chosen, propagator, precision=lax.Precision.HIGHEST)
    mean_square = lax.optimization_barrier(jnp.mean(propagated * propagated, axis=(1, 2)))
    current = propagated / jnp.sqrt(mean_square + epsilon)[:, None, None]
    for repeat_index in range(NS_ITERS):
        intersection = jnp.einsum('wjp,wkp->wjk', current, current, precision=lax.Precision.HIGHEST) / NORB
        current = 0.5 * (3.0 * current - jnp.einsum('wjk,wkp->wjp', intersection, current, precision=lax.Precision.HIGHEST))
    return (current, new_log_weights)
```

```python
import functools
import math

import jax
import jax.numpy as jnp
from jax import lax
from jax.experimental import pallas as pl
from jax.experimental.pallas import tpu as pltpu
from jax.sharding import PartitionSpec as P

NS_ITERS = 2
EXTRA = 16

gradient_step = 0.25
energy_step = 0.002
epsilon = 1e-06

VMEM_LIMIT = 32 * 1024 * 1024


def call(body, out_shape, in_specs, out_specs, scratch=()):
    return pl.pallas_call(
        body,
        out_shape=out_shape,
        in_specs=in_specs,
        out_specs=out_specs,
        scratch_shapes=list(scratch),
        compiler_params=pltpu.CompilerParams(vmem_limit_bytes=VMEM_LIMIT),
    )


def vmem(count):
    return [pl.BlockSpec(memory_space=pltpu.VMEM)] * count


def swap(array, axis, partner):
    size = lax.axis_size(axis)
    return lax.ppermute(array, axis, [(i, partner(i)) for i in range(size)])


def select_kernel(parent_ref, *refs):
    *row_refs, theta_ref, extra_ref = refs
    occupied = theta_ref.shape[0]
    place = jnp.bitwise_xor(parent_ref[0], lax.axis_index("wlk"))
    for index, ref in enumerate(row_refs):

        @pl.when(place == index)
        def _():
            theta_ref[...] = ref[:occupied, :]
            extra_ref[...] = ref[occupied:, :]


def gradient_kernel(norm_scale, blocks, summands, theta_ref, *refs):
    chol_refs = refs[:blocks]
    sum_refs = refs[blocks : blocks + summands]
    out_ref, adjoint = refs[blocks + summands :]
    occupied = theta_ref.shape[0]
    theta = theta_ref[...]
    rows = lax.broadcasted_iota(jnp.int32, (occupied, occupied), 0)
    columns = lax.broadcasted_iota(jnp.int32, (occupied, occupied), 1)
    diagonal = rows == columns
    total = None
    for ref in sum_refs:
        term = ref[...].astype(jnp.float32)
        total = term if total is None else total + term
    for ref in chol_refs:
        vectors, _, basis = ref.shape
        chol = ref[...].reshape(vectors * occupied, basis)
        turned = lax.dot_general(
            chol, theta, (((1,), (1,)), ((), ())), preferred_element_type=jnp.float32
        )
        turned = turned.astype(jnp.bfloat16).astype(jnp.float32)
        for g in range(vectors):
            block = turned[g * occupied : (g + 1) * occupied, :]
            on_diagonal = jnp.where(diagonal, block, 0.0)
            trace = jnp.sum(jnp.sum(on_diagonal, axis=0, keepdims=True), axis=1, keepdims=True)
            piece = norm_scale * (jnp.where(diagonal, trace, 0.0) - block)
            adjoint[:, g * occupied : (g + 1) * occupied] = piece.astype(jnp.bfloat16)
        term = jnp.dot(
            adjoint[:, : vectors * occupied], chol, preferred_element_type=jnp.float32
        )
        total = term if total is None else total + term
    out_ref[...] = total.astype(out_ref.dtype)


def partial_gradient(norm_scale, theta, chols, summands, dtype):
    occupied, basis = theta.shape
    most = max(c.shape[0] for c in chols)
    return call(
        functools.partial(gradient_kernel, norm_scale, len(chols), len(summands)),
        jax.ShapeDtypeStruct((occupied, basis), dtype),
        vmem(1 + len(chols) + len(summands)),
        pl.BlockSpec(memory_space=pltpu.VMEM),
        [pltpu.VMEM((occupied, most * occupied), jnp.bfloat16)],
    )(theta, *chols, *summands)


def final_kernel(theta_ref, extra_ref, own_ref, other_ref, propagator_ref, out_ref, log_ref):
    occupied, basis = theta_ref.shape
    theta = theta_ref[...].astype(jnp.float32)
    gradient = own_ref[...] + other_ref[...].astype(jnp.float32)
    energy = 0.5 * jnp.sum(theta * gradient)
    log_weight = jnp.sum(extra_ref[...].astype(jnp.float32))
    log_ref[0] = log_weight - energy_step * energy
    stepped = (theta - gradient_step * gradient).astype(jnp.bfloat16)
    propagated = lax.dot_general(
        stepped, propagator_ref[...], (((1,), (1,)), ((), ())), preferred_element_type=jnp.float32
    )
    mean_square = jnp.sum(propagated * propagated, keepdims=True) / (occupied * basis)
    current = propagated * lax.rsqrt(mean_square + epsilon)
    for _ in range(NS_ITERS):
        narrow = current.astype(jnp.bfloat16)
        overlap = lax.dot_general(
            narrow, narrow, (((1,), (1,)), ((), ())), preferred_element_type=jnp.float32
        )
        overlap = (overlap * (0.5 / basis)).astype(jnp.bfloat16)
        current = 1.5 * current - jnp.dot(overlap, narrow, preferred_element_type=jnp.float32)
    out_ref[...] = current


def local(cholesky, orbitals, log_weights, parents, propagator):
    walker_count, occupied, basis = orbitals.shape
    vectors_here = cholesky.shape[0]
    vec_size, wlk_size = lax.axis_size("vec"), lax.axis_size("wlk")
    norm_scale = 1.0 / math.sqrt(vectors_here * vec_size)
    half = vectors_here // 2
    core = lax.axis_index("wlk") % 2

    mine = lax.dynamic_slice_in_dim(cholesky, core * half, half, 0)
    cross = [
        lax.ppermute(mine, "vec", [(i, (i + 2 * m) % vec_size) for i in range(vec_size)])
        for m in range(1, vec_size // 2)
    ]

    theta = orbitals[0].astype(jnp.bfloat16)
    high = log_weights.astype(jnp.bfloat16)
    rest = log_weights - high.astype(jnp.float32)
    middle = rest.astype(jnp.bfloat16)
    low = (rest - middle.astype(jnp.float32)).astype(jnp.bfloat16)
    extra = jnp.concatenate([high, middle, low]).reshape(1, 3)
    extra = jnp.pad(extra, ((0, EXTRA - 1), (0, basis - 3)))
    payload = jnp.concatenate([theta, extra], axis=0)

    row = [payload] + [swap(payload, "wlk", lambda i, m=m: i ^ (2 * m)) for m in range(1, wlk_size // 2)]
    across = swap(jnp.stack(row), "wlk", lambda i: i ^ 1)
    row = [r for m in range(wlk_size // 2) for r in (row[m], across[m])]

    smem = pl.BlockSpec(memory_space=pltpu.SMEM)
    chosen, chosen_extra = call(
        select_kernel,
        (
            jax.ShapeDtypeStruct((occupied, basis), jnp.bfloat16),
            jax.ShapeDtypeStruct((EXTRA, basis), jnp.bfloat16),
        ),
        [smem] + vmem(wlk_size),
        vmem(2),
    )(parents, *row)
    neighbour = swap(chosen, "vec", lambda i: i ^ 1)

    other = [swap(c, "wlk", lambda i: i ^ 1) for c in cross]
    own_part = partial_gradient(norm_scale, chosen, [cholesky], [], jnp.float32)
    to_send = partial_gradient(norm_scale, neighbour, [cholesky, *cross], [], jnp.float32)
    to_send = partial_gradient(norm_scale, neighbour, other, [to_send], jnp.bfloat16)
    received = swap(to_send, "vec", lambda i: i ^ 1)
    own_part = partial_gradient(norm_scale, chosen, [*cross, *other], [own_part], jnp.float32)

    new_orbitals, new_logs = call(
        final_kernel,
        (
            jax.ShapeDtypeStruct((occupied, basis), jnp.float32),
            jax.ShapeDtypeStruct((1,), jnp.float32),
        ),
        vmem(5),
        [pl.BlockSpec(memory_space=pltpu.VMEM), smem],
    )(chosen, chosen_extra, own_part, received, propagator.astype(jnp.bfloat16))
    return new_orbitals.reshape(orbitals.shape), new_logs


def solution(mesh):
    placed = (
        P(("grp", "vec"), None, None),
        P(("grp", "vec", "wlk"), None, None),
        P(("grp", "vec", "wlk")),
        P(("grp", "vec", "wlk")),
        P("grp", None),
    )
    return jax.shard_map(
        local,
        mesh=mesh,
        in_specs=placed,
        out_specs=(P(("grp", "vec", "wlk"), None, None), P(("grp", "vec", "wlk"))),
        check_vma=False,
    )
```

```python
import functools
import math

import jax
import jax.numpy as jnp
from jax import lax
from jax.experimental import pallas as pl
from jax.experimental.pallas import tpu as pltpu
from jax.sharding import PartitionSpec as P

NS_ITERS = 2
EXTRA = 16

gradient_step = 0.25
energy_step = 0.002
epsilon = 1e-06

VMEM_LIMIT = 32 * 1024 * 1024


def call(body, out_shape, in_specs, out_specs, scratch=()):
    return pl.pallas_call(
        body,
        out_shape=out_shape,
        in_specs=in_specs,
        out_specs=out_specs,
        scratch_shapes=list(scratch),
        compiler_params=pltpu.CompilerParams(vmem_limit_bytes=VMEM_LIMIT),
    )


def vmem(count):
    return [pl.BlockSpec(memory_space=pltpu.VMEM)] * count


def swap(array, axis, partner):
    size = lax.axis_size(axis)
    return lax.ppermute(array, axis, [(i, partner(i)) for i in range(size)])


def payload_kernel(log_ref, parent_ref, orbitals_ref, payload_ref, place_ref):
    occupied, basis = orbitals_ref.shape[1:]
    parent = jnp.broadcast_to(parent_ref[...].reshape(1, 1), place_ref.shape)
    place_ref[...] = parent
    value = jnp.broadcast_to(log_ref[...].reshape(1, 1), (EXTRA, basis))
    high = value.astype(jnp.bfloat16).astype(jnp.float32)
    middle = (value - high).astype(jnp.bfloat16).astype(jnp.float32)
    low = value - high - middle
    rows = lax.broadcasted_iota(jnp.int32, (EXTRA, basis), 0)
    lanes = lax.broadcasted_iota(jnp.int32, (EXTRA, basis), 1)
    pieces = jnp.where(rows == 0, high, jnp.where(rows == 1, middle, jnp.where(rows == 2, low, 0.0)))
    payload_ref[occupied:, :] = jnp.where(lanes == 0, pieces, 0.0).astype(jnp.bfloat16)
    payload_ref[:occupied, :] = orbitals_ref[0].astype(jnp.bfloat16)


def select_kernel(place_ref, *refs):
    *row_refs, theta_ref, extra_ref = refs
    occupied, basis = theta_ref.shape
    whole = (occupied + EXTRA, basis)
    place = jnp.broadcast_to(place_ref[:1, :1], whole)
    picked = row_refs[0][...].astype(jnp.float32)
    for index, ref in enumerate(row_refs[1:]):
        picked = jnp.where(place == index + 1, ref[...].astype(jnp.float32), picked)
    picked = picked.astype(jnp.bfloat16)
    theta_ref[...] = picked[:occupied]
    extra_ref[...] = picked[occupied:]


def gradient_kernel(norm_scale, blocks, summands, theta_ref, *refs):
    chol_refs = refs[:blocks]
    sum_refs = refs[blocks : blocks + summands]
    out_ref, adjoint = refs[blocks + summands :]
    occupied = theta_ref.shape[0]
    theta = theta_ref[...]
    rows = lax.broadcasted_iota(jnp.int32, (occupied, occupied), 0)
    columns = lax.broadcasted_iota(jnp.int32, (occupied, occupied), 1)
    diagonal = rows == columns
    total = None
    for ref in sum_refs:
        term = ref[...].astype(jnp.float32)
        total = term if total is None else total + term
    for ref in chol_refs:
        vectors, _, basis = ref.shape
        chol = ref[...].reshape(vectors * occupied, basis)
        turned = lax.dot_general(
            chol, theta, (((1,), (1,)), ((), ())), preferred_element_type=jnp.float32
        )
        turned = turned.astype(jnp.bfloat16).astype(jnp.float32)
        for g in range(vectors):
            block = turned[g * occupied : (g + 1) * occupied, :]
            on_diagonal = jnp.where(diagonal, block, 0.0)
            trace = jnp.sum(jnp.sum(on_diagonal, axis=0, keepdims=True), axis=1, keepdims=True)
            piece = norm_scale * (jnp.where(diagonal, trace, 0.0) - block)
            adjoint[:, g * occupied : (g + 1) * occupied] = piece.astype(jnp.bfloat16)
        term = jnp.dot(
            adjoint[:, : vectors * occupied], chol, preferred_element_type=jnp.float32
        )
        total = term if total is None else total + term
    out_ref[...] = total.astype(out_ref.dtype)


def partial_gradient(norm_scale, theta, chols, summands, dtype):
    occupied, basis = theta.shape
    most = max(c.shape[0] for c in chols)
    return call(
        functools.partial(gradient_kernel, norm_scale, len(chols), len(summands)),
        jax.ShapeDtypeStruct((occupied, basis), dtype),
        vmem(1 + len(chols) + len(summands)),
        pl.BlockSpec(memory_space=pltpu.VMEM),
        [pltpu.VMEM((occupied, most * occupied), jnp.bfloat16)],
    )(theta, *chols, *summands)


def final_kernel(theta_ref, extra_ref, own_ref, other_ref, propagator_ref, out_ref, log_ref):
    occupied, basis = theta_ref.shape
    theta = theta_ref[...].astype(jnp.float32)
    gradient = own_ref[...] + other_ref[...].astype(jnp.float32)
    energy = 0.5 * jnp.sum(theta * gradient)
    log_weight = jnp.sum(extra_ref[...].astype(jnp.float32))
    log_ref[0] = log_weight - energy_step * energy
    stepped = (theta - gradient_step * gradient).astype(jnp.bfloat16)
    propagated = lax.dot_general(
        stepped, propagator_ref[...], (((1,), (1,)), ((), ())), preferred_element_type=jnp.float32
    )
    mean_square = jnp.sum(propagated * propagated, keepdims=True) / (occupied * basis)
    current = propagated * lax.rsqrt(mean_square + epsilon)
    for _ in range(NS_ITERS):
        narrow = current.astype(jnp.bfloat16)
        overlap = lax.dot_general(
            narrow, narrow, (((1,), (1,)), ((), ())), preferred_element_type=jnp.float32
        )
        overlap = (overlap * (0.5 / basis)).astype(jnp.bfloat16)
        current = 1.5 * current - jnp.dot(overlap, narrow, preferred_element_type=jnp.float32)
    out_ref[...] = current


def local(cholesky, orbitals, log_weights, parents, propagator):
    walker_count, occupied, basis = orbitals.shape
    vectors_here = cholesky.shape[0]
    vec_size, wlk_size = lax.axis_size("vec"), lax.axis_size("wlk")
    norm_scale = 1.0 / math.sqrt(vectors_here * vec_size)
    half = vectors_here // 2
    smem = pl.BlockSpec(memory_space=pltpu.SMEM)

    here = lax.axis_index("wlk")
    mine = lax.dynamic_slice_in_dim(cholesky, here % 2 * half, half, 0)

    cross = [
        lax.ppermute(mine, "vec", [(i, (i + 2 * m) % vec_size) for i in range(vec_size)])
        for m in range(1, vec_size // 2)
    ]


    def walkers(orbitals, log_weights, parents):
        payload, place = call(
            payload_kernel,
            (
                jax.ShapeDtypeStruct((occupied + EXTRA, basis), jnp.bfloat16),
                jax.ShapeDtypeStruct((8, 128), jnp.int32),
            ),
            vmem(3),
            vmem(2),
        )(log_weights, parents, orbitals)
        gathered = lax.all_gather(payload, "wlk", axis=0)
        row = [gathered[m] for m in range(wlk_size)]
        chosen, chosen_extra = call(
            select_kernel,
            (
                jax.ShapeDtypeStruct((occupied, basis), jnp.bfloat16),
                jax.ShapeDtypeStruct((EXTRA, basis), jnp.bfloat16),
            ),
            vmem(1 + wlk_size),
            vmem(2),
        )(place, *row)
        return chosen, chosen_extra, swap(chosen, "vec", lambda i: i ^ 1)

    chosen, chosen_extra, neighbour = walkers(orbitals, log_weights, parents)
    *cross, neighbour = lax.optimization_barrier((*cross, neighbour))
    other = [swap(c, "wlk", lambda i: i ^ 1) for c in cross]
    own_part = partial_gradient(norm_scale, chosen, [cholesky], [], jnp.float32)
    to_send = partial_gradient(norm_scale, neighbour, [cholesky, *cross], [], jnp.float32)
    to_send = partial_gradient(norm_scale, neighbour, other, [to_send], jnp.bfloat16)
    received = swap(to_send, "vec", lambda i: i ^ 1)
    own_part = partial_gradient(norm_scale, chosen, [*cross, *other], [own_part], jnp.float32)

    new_orbitals, new_logs = call(
        final_kernel,
        (
            jax.ShapeDtypeStruct((occupied, basis), jnp.float32),
            jax.ShapeDtypeStruct((1,), jnp.float32),
        ),
        vmem(5),
        [pl.BlockSpec(memory_space=pltpu.VMEM), smem],
    )(chosen, chosen_extra, own_part, received, propagator.astype(jnp.bfloat16))
    return new_orbitals.reshape(orbitals.shape), new_logs


def solution(mesh):
    placed = (
        P(("grp", "vec"), None, None),
        P(("grp", "vec", "wlk"), None, None),
        P(("grp", "vec", "wlk")),
        P(("grp", "vec", "wlk")),
        P("grp", None),
    )
    return jax.shard_map(
        local,
        mesh=mesh,
        in_specs=placed,
        out_specs=(P(("grp", "vec", "wlk"), None, None), P(("grp", "vec", "wlk"))),
        check_vma=False,
    )
```

```python
import functools
import math

import jax
import jax.numpy as jnp
from jax import lax
from jax.experimental import pallas as pl
from jax.experimental.pallas import tpu as pltpu
from jax.sharding import PartitionSpec as P

NS_ITERS = 2
EXTRA = 16

gradient_step = 0.25
energy_step = 0.002
epsilon = 1e-06

VMEM_LIMIT = 32 * 1024 * 1024


def call(body, out_shape, in_specs, out_specs, scratch=(), cost=None):
    return pl.pallas_call(
        body,
        out_shape=out_shape,
        in_specs=in_specs,
        out_specs=out_specs,
        scratch_shapes=list(scratch),
        cost_estimate=cost,
        compiler_params=pltpu.CompilerParams(vmem_limit_bytes=VMEM_LIMIT),
    )


def vmem(count):
    return [pl.BlockSpec(memory_space=pltpu.VMEM)] * count


def swap(array, axis, partner):
    size = lax.axis_size(axis)
    return lax.ppermute(array, axis, [(i, partner(i)) for i in range(size)])


def blank_kernel(out_ref):
    out_ref[...] = jnp.zeros(out_ref.shape, out_ref.dtype)


def tile_kernel(log_ref, parent_ref, blank_ref, out_ref):
    rows = lax.broadcasted_iota(jnp.int32, out_ref.shape, 0)
    out_ref[...] = jnp.where(rows == 0, log_ref[0], parent_ref[0].astype(jnp.float32))


def half_kernel(tile_ref, chol_ref, out_ref):
    half = out_ref.shape[0]
    out_ref[...] = chol_ref[pl.ds(lax.rem(lax.axis_index("wlk"), 2) * half, half)]


def payload_kernel(tile_ref, orbitals_ref, payload_ref):
    occupied = orbitals_ref.shape[1]
    payload_ref[:occupied, :] = orbitals_ref[0].astype(jnp.bfloat16)
    value = jnp.broadcast_to(tile_ref[0:1, :], payload_ref[occupied:, :].shape)
    high = value.astype(jnp.bfloat16).astype(jnp.float32)
    middle = (value - high).astype(jnp.bfloat16).astype(jnp.float32)
    low = value - high - middle
    rows = lax.broadcasted_iota(jnp.int32, value.shape, 0)
    lanes = lax.broadcasted_iota(jnp.int32, value.shape, 1)
    pieces = jnp.where(rows == 0, high, jnp.where(rows == 1, middle, jnp.where(rows == 2, low, 0.0)))
    payload_ref[occupied:, :] = jnp.where(lanes == 0, pieces, 0.0).astype(jnp.bfloat16)


def select_kernel(tile_ref, *refs):
    *row_refs, theta_ref, extra_ref = refs
    occupied, basis = theta_ref.shape
    whole = (occupied + EXTRA, basis)
    place = jnp.broadcast_to(tile_ref[1:2, :], whole).astype(jnp.int32)
    picked = row_refs[0][...].astype(jnp.float32)
    for index, ref in enumerate(row_refs[1:]):
        picked = jnp.where(place == index + 1, ref[...].astype(jnp.float32), picked)
    picked = picked.astype(jnp.bfloat16)
    theta_ref[...] = picked[:occupied]
    extra_ref[...] = picked[occupied:]


def gradient_kernel(norm_scale, blocks, summands, theta_ref, *refs):
    chol_refs = refs[:blocks]
    sum_refs = refs[blocks : blocks + summands]
    out_ref, adjoint = refs[blocks + summands :]
    occupied, basis = theta_ref.shape
    theta = theta_ref[...]
    rows = lax.broadcasted_iota(jnp.int32, (occupied, occupied), 0)
    columns = lax.broadcasted_iota(jnp.int32, (occupied, occupied), 1)
    diagonal = rows == columns
    turned = [
        lax.dot_general(
            ref[...].reshape(-1, basis), theta, (((1,), (1,)), ((), ())),
            preferred_element_type=jnp.float32,
        )
        for ref in chol_refs
    ]
    place = 0
    for product in turned:
        product = product.astype(jnp.bfloat16).astype(jnp.float32)
        for g in range(product.shape[0] // occupied):
            block = product[g * occupied : (g + 1) * occupied, :]
            on_diagonal = jnp.where(diagonal, block, 0.0)
            trace = jnp.sum(jnp.sum(on_diagonal, axis=0, keepdims=True), axis=1, keepdims=True)
            piece = norm_scale * (jnp.where(diagonal, trace, 0.0) - block)
            adjoint[:, place : place + occupied] = piece.astype(jnp.bfloat16)
            place += occupied
    total = None
    for ref in sum_refs:
        term = ref[...].astype(jnp.float32)
        total = term if total is None else total + term
    place = 0
    for ref in chol_refs:
        width = ref.shape[0] * occupied
        term = jnp.dot(
            adjoint[:, place : place + width], ref[...].reshape(-1, basis),
            preferred_element_type=jnp.float32,
        )
        total = term if total is None else total + term
        place += width
    out_ref[...] = total.astype(out_ref.dtype)


def partial_gradient(norm_scale, theta, chols, summands, dtype, cost=None):
    occupied, basis = theta.shape
    width = sum(c.shape[0] for c in chols) * occupied
    return call(
        functools.partial(gradient_kernel, norm_scale, len(chols), len(summands)),
        jax.ShapeDtypeStruct((occupied, basis), dtype),
        vmem(1 + len(chols) + len(summands)),
        pl.BlockSpec(memory_space=pltpu.VMEM),
        [pltpu.VMEM((occupied, width), jnp.bfloat16)],
        cost,
    )(theta, *chols, *summands)


def final_kernel(theta_ref, extra_ref, own_ref, other_ref, propagator_ref, out_ref, log_ref):
    occupied, basis = theta_ref.shape
    theta = theta_ref[...].astype(jnp.float32)
    gradient = own_ref[...] + other_ref[...].astype(jnp.float32)
    energy = 0.5 * jnp.sum(theta * gradient)
    log_weight = jnp.sum(extra_ref[...].astype(jnp.float32))
    log_ref[0] = log_weight - energy_step * energy
    stepped = (theta - gradient_step * gradient).astype(jnp.bfloat16)
    propagated = lax.dot_general(
        stepped, propagator_ref[...], (((1,), (1,)), ((), ())), preferred_element_type=jnp.float32
    )
    mean_square = jnp.sum(propagated * propagated, keepdims=True) / (occupied * basis)
    current = propagated * lax.rsqrt(mean_square + epsilon)
    for _ in range(NS_ITERS):
        narrow = current.astype(jnp.bfloat16)
        overlap = lax.dot_general(
            narrow, narrow, (((1,), (1,)), ((), ())), preferred_element_type=jnp.float32
        )
        overlap = (overlap * (0.5 / basis)).astype(jnp.bfloat16)
        current = 1.5 * current - jnp.dot(overlap, narrow, preferred_element_type=jnp.float32)
    out_ref[...] = current


def local(cholesky, orbitals, log_weights, parents, propagator):
    walker_count, occupied, basis = orbitals.shape
    vectors_here = cholesky.shape[0]
    vec_size, wlk_size = lax.axis_size("vec"), lax.axis_size("wlk")
    norm_scale = 1.0 / math.sqrt(vectors_here * vec_size)
    half = vectors_here // 2
    smem = pl.BlockSpec(memory_space=pltpu.SMEM)

    here = lax.axis_index("wlk")
    blank = call(
        blank_kernel,
        jax.ShapeDtypeStruct((8, basis), jnp.float32),
        [],
        vmem(1)[0],
        (),
        pl.CostEstimate(flops=10**11, bytes_accessed=256 * 2**20, transcendentals=0),
    )()
    tile = call(
        tile_kernel,
        jax.ShapeDtypeStruct((8, basis), jnp.float32),
        [smem] * 2 + vmem(1),
        vmem(1)[0],
    )(log_weights, parents, blank)
    mine = call(
        half_kernel,
        jax.ShapeDtypeStruct((half, occupied, basis), cholesky.dtype),
        vmem(2),
        vmem(1)[0],
    )(tile, cholesky)

    cross = [
        lax.ppermute(mine, "vec", [(i, (i + 2 * m) % vec_size) for i in range(vec_size)])
        for m in range(1, vec_size // 2)
    ]


    def walkers(orbitals, log_weights, parents):
        payload = call(
            payload_kernel,
            jax.ShapeDtypeStruct((occupied + EXTRA, basis), jnp.bfloat16),
            vmem(2),
            vmem(1)[0],
        )(tile, orbitals)
        gathered = lax.all_gather(payload, "wlk", axis=0)
        row = [gathered[m] for m in range(wlk_size)]
        chosen, chosen_extra = call(
            select_kernel,
            (
                jax.ShapeDtypeStruct((occupied, basis), jnp.bfloat16),
                jax.ShapeDtypeStruct((EXTRA, basis), jnp.bfloat16),
            ),
            vmem(1 + wlk_size),
            vmem(2),
        )(tile, *row)
        return chosen, chosen_extra, swap(chosen, "vec", lambda i: i ^ 1)

    chosen, chosen_extra, neighbour = walkers(orbitals, log_weights, parents)
    *cross, chosen = lax.optimization_barrier((*cross, chosen))
    other = [swap(c, "wlk", lambda i: i ^ 1) for c in cross]
    slow = pl.CostEstimate(flops=10**11, bytes_accessed=256 * 2**20, transcendentals=0)
    own_part = partial_gradient(norm_scale, chosen, [cholesky], [], jnp.float32)
    to_send = partial_gradient(norm_scale, neighbour, [cholesky], [], jnp.float32, slow)
    to_send = partial_gradient(norm_scale, neighbour, [*cross, *other], [to_send], jnp.bfloat16)
    received = swap(to_send, "vec", lambda i: i ^ 1)
    own_part = partial_gradient(norm_scale, chosen, [*cross, *other], [own_part], jnp.float32)

    new_orbitals, new_logs = call(
        final_kernel,
        (
            jax.ShapeDtypeStruct((occupied, basis), jnp.float32),
            jax.ShapeDtypeStruct((1,), jnp.float32),
        ),
        vmem(5),
        [pl.BlockSpec(memory_space=pltpu.VMEM), smem],
    )(chosen, chosen_extra, own_part, received, propagator.astype(jnp.bfloat16))
    return new_orbitals.reshape(orbitals.shape), new_logs


def solution(mesh):
    placed = (
        P(("grp", "vec"), None, None),
        P(("grp", "vec", "wlk"), None, None),
        P(("grp", "vec", "wlk")),
        P(("grp", "vec", "wlk")),
        P("grp", None),
    )
    return jax.shard_map(
        local,
        mesh=mesh,
        in_specs=placed,
        out_specs=(P(("grp", "vec", "wlk"), None, None), P(("grp", "vec", "wlk"))),
        check_vma=False,
    )
```

```python
import functools
import math

import jax
import jax.numpy as jnp
from jax import lax
from jax.experimental import pallas as pl
from jax.experimental.pallas import tpu as pltpu
from jax.sharding import PartitionSpec as P

NS_ITERS = 2
EXTRA = 16

gradient_step = 0.25
energy_step = 0.002
epsilon = 1e-06

VMEM_LIMIT = 32 * 1024 * 1024


def call(body, out_shape, in_specs, out_specs, scratch=(), cost=None):
    return pl.pallas_call(
        body,
        out_shape=out_shape,
        in_specs=in_specs,
        out_specs=out_specs,
        scratch_shapes=list(scratch),
        cost_estimate=cost,
        compiler_params=pltpu.CompilerParams(vmem_limit_bytes=VMEM_LIMIT),
    )


def vmem(count):
    return [pl.BlockSpec(memory_space=pltpu.VMEM)] * count


def swap(array, axis, partner):
    size = lax.axis_size(axis)
    return lax.ppermute(array, axis, [(i, partner(i)) for i in range(size)])


def blank_kernel(out_ref):
    out_ref[...] = jnp.zeros(out_ref.shape, out_ref.dtype)


def tile_kernel(log_ref, parent_ref, blank_ref, out_ref):
    rows = lax.broadcasted_iota(jnp.int32, out_ref.shape, 0)
    out_ref[...] = jnp.where(rows == 0, log_ref[0], parent_ref[0].astype(jnp.float32))


def half_kernel(tile_ref, chol_ref, out_ref):
    half = out_ref.shape[0]
    out_ref[...] = chol_ref[pl.ds(lax.rem(lax.axis_index("wlk"), 2) * half, half)]


def payload_kernel(tile_ref, orbitals_ref, payload_ref):
    occupied = orbitals_ref.shape[1]
    payload_ref[:occupied, :] = orbitals_ref[0].astype(jnp.bfloat16)
    value = jnp.broadcast_to(tile_ref[0:1, :], payload_ref[occupied:, :].shape)
    high = value.astype(jnp.bfloat16).astype(jnp.float32)
    middle = (value - high).astype(jnp.bfloat16).astype(jnp.float32)
    low = value - high - middle
    rows = lax.broadcasted_iota(jnp.int32, value.shape, 0)
    lanes = lax.broadcasted_iota(jnp.int32, value.shape, 1)
    pieces = jnp.where(rows == 0, high, jnp.where(rows == 1, middle, jnp.where(rows == 2, low, 0.0)))
    payload_ref[occupied:, :] = jnp.where(lanes == 0, pieces, 0.0).astype(jnp.bfloat16)


def select_kernel(tile_ref, *refs):
    *row_refs, theta_ref, extra_ref = refs
    occupied, basis = theta_ref.shape
    whole = (occupied + EXTRA, basis)
    place = jnp.broadcast_to(tile_ref[1:2, :], whole).astype(jnp.int32)
    picked = row_refs[0][...].astype(jnp.float32)
    for index, ref in enumerate(row_refs[1:]):
        picked = jnp.where(place == index + 1, ref[...].astype(jnp.float32), picked)
    picked = picked.astype(jnp.bfloat16)
    theta_ref[...] = picked[:occupied]
    extra_ref[...] = picked[occupied:]


def copy_kernel(in_ref, out_ref):
    out_ref[...] = in_ref[...]


def gradient_kernel(norm_scale, theta_ref, *refs):
    *chol_refs, out_ref, adjoint = refs
    occupied, basis = theta_ref.shape
    theta = theta_ref[...]
    rows = lax.broadcasted_iota(jnp.int32, (occupied, occupied), 0)
    columns = lax.broadcasted_iota(jnp.int32, (occupied, occupied), 1)
    diagonal = rows == columns
    turned = [
        lax.dot_general(
            ref[...].reshape(-1, basis), theta, (((1,), (1,)), ((), ())),
            preferred_element_type=jnp.float32,
        )
        for ref in chol_refs
    ]
    place = 0
    for product in turned:
        product = product.astype(jnp.bfloat16).astype(jnp.float32)
        for g in range(product.shape[0] // occupied):
            block = product[g * occupied : (g + 1) * occupied, :]
            on_diagonal = jnp.where(diagonal, block, 0.0)
            trace = jnp.sum(jnp.sum(on_diagonal, axis=0, keepdims=True), axis=1, keepdims=True)
            piece = norm_scale * (jnp.where(diagonal, trace, 0.0) - block)
            adjoint[:, place : place + occupied] = piece.astype(jnp.bfloat16)
            place += occupied
    total = None
    place = 0
    for ref in chol_refs:
        width = ref.shape[0] * occupied
        term = jnp.dot(
            adjoint[:, place : place + width], ref[...].reshape(-1, basis),
            preferred_element_type=jnp.float32,
        )
        total = term if total is None else total + term
        place += width
    out_ref[...] = total.astype(out_ref.dtype)


def partial_gradient(norm_scale, theta, chols, dtype):
    occupied, basis = theta.shape
    width = sum(c.shape[0] for c in chols) * occupied
    return call(
        functools.partial(gradient_kernel, norm_scale),
        jax.ShapeDtypeStruct((occupied, basis), dtype),
        vmem(1 + len(chols)),
        pl.BlockSpec(memory_space=pltpu.VMEM),
        [pltpu.VMEM((occupied, width), jnp.bfloat16)],
    )(theta, *chols)


def final_kernel(theta_ref, extra_ref, own_ref, other_ref, propagator_ref, out_ref, log_ref):
    occupied, basis = theta_ref.shape
    theta = theta_ref[...].astype(jnp.float32)
    gradient = own_ref[...] + other_ref[...].astype(jnp.float32)
    energy = 0.5 * jnp.sum(theta * gradient)
    log_weight = jnp.sum(extra_ref[...].astype(jnp.float32))
    log_ref[0] = log_weight - energy_step * energy
    stepped = (theta - gradient_step * gradient).astype(jnp.bfloat16)
    propagated = jnp.dot(stepped, propagator_ref[...], preferred_element_type=jnp.float32)
    narrow = propagated.astype(jnp.bfloat16)
    overlap = lax.dot_general(
        narrow, narrow, (((1,), (1,)), ((), ())), preferred_element_type=jnp.float32
    )
    diagonal = lax.broadcasted_iota(jnp.int32, overlap.shape, 0) == lax.broadcasted_iota(
        jnp.int32, overlap.shape, 1
    )
    squares = jnp.sum(jnp.where(diagonal, overlap, 0.0), keepdims=True)
    scale = lax.rsqrt(squares / (occupied * basis) + epsilon)
    overlap = overlap * scale * (scale * (0.5 / basis))
    current = propagated * scale
    for index in range(NS_ITERS):
        if index:
            narrow = current.astype(jnp.bfloat16)
            overlap = lax.dot_general(
                narrow, narrow, (((1,), (1,)), ((), ())), preferred_element_type=jnp.float32
            ) * (0.5 / basis)
        else:
            narrow = current.astype(jnp.bfloat16)
        current = 1.5 * current - jnp.dot(
            overlap.astype(jnp.bfloat16), narrow, preferred_element_type=jnp.float32
        )
    out_ref[...] = current


def local(cholesky, orbitals, log_weights, parents, propagator):
    walker_count, occupied, basis = orbitals.shape
    vectors_here = cholesky.shape[0]
    vec_size, wlk_size = lax.axis_size("vec"), lax.axis_size("wlk")
    norm_scale = 1.0 / math.sqrt(vectors_here * vec_size)
    half = vectors_here // 2
    smem = pl.BlockSpec(memory_space=pltpu.SMEM)

    here = lax.axis_index("wlk")
    blank = call(
        blank_kernel,
        jax.ShapeDtypeStruct((8, basis), jnp.float32),
        [],
        vmem(1)[0],
        (),
        pl.CostEstimate(flops=10**11, bytes_accessed=256 * 2**20, transcendentals=0),
    )()
    tile = call(
        tile_kernel,
        jax.ShapeDtypeStruct((8, basis), jnp.float32),
        [smem] * 2 + vmem(1),
        vmem(1)[0],
    )(log_weights, parents, blank)
    mine = call(
        half_kernel,
        jax.ShapeDtypeStruct((half, occupied, basis), cholesky.dtype),
        vmem(2),
        vmem(1)[0],
    )(tile, cholesky)

    cross = [
        lax.ppermute(mine, "vec", [(i, (i + 2 * m) % vec_size) for i in range(vec_size)])
        for m in range(1, vec_size // 2)
    ]


    def walkers(orbitals, log_weights, parents):
        payload = call(
            payload_kernel,
            jax.ShapeDtypeStruct((occupied + EXTRA, basis), jnp.bfloat16),
            vmem(2),
            vmem(1)[0],
        )(tile, orbitals)
        gathered = lax.all_gather(payload, "wlk", axis=0)
        row = [gathered[m] for m in range(wlk_size)]
        chosen, chosen_extra = call(
            select_kernel,
            (
                jax.ShapeDtypeStruct((occupied, basis), jnp.bfloat16),
                jax.ShapeDtypeStruct((EXTRA, basis), jnp.bfloat16),
            ),
            vmem(1 + wlk_size),
            vmem(2),
        )(tile, *row)
        return chosen, chosen_extra, swap(chosen, "vec", lambda i: i ^ 1)

    chosen, chosen_extra, neighbour = walkers(orbitals, log_weights, parents)
    *cross, chosen = lax.optimization_barrier((*cross, chosen))
    other = [swap(c, "wlk", lambda i: i ^ 1) for c in cross]
    slow = pl.CostEstimate(flops=10**11, bytes_accessed=256 * 2**20, transcendentals=0)
    arrived = call(
        copy_kernel,
        jax.ShapeDtypeStruct(neighbour.shape, neighbour.dtype),
        vmem(1),
        vmem(1)[0],
        (),
        slow,
    )(neighbour)
    vectors = [cholesky, *cross, *other]
    to_send = partial_gradient(norm_scale, arrived, vectors, jnp.bfloat16)
    received = swap(to_send, "vec", lambda i: i ^ 1)
    own_part = partial_gradient(norm_scale, chosen, vectors, jnp.float32)

    new_orbitals, new_logs = call(
        final_kernel,
        (
            jax.ShapeDtypeStruct((occupied, basis), jnp.float32),
            jax.ShapeDtypeStruct((1,), jnp.float32),
        ),
        vmem(5),
        [pl.BlockSpec(memory_space=pltpu.VMEM), smem],
    )(chosen, chosen_extra, own_part, received, propagator.T.astype(jnp.bfloat16))
    return new_orbitals.reshape(orbitals.shape), new_logs


def solution(mesh):
    placed = (
        P(("grp", "vec"), None, None),
        P(("grp", "vec", "wlk"), None, None),
        P(("grp", "vec", "wlk")),
        P(("grp", "vec", "wlk")),
        P("grp", None),
    )
    return jax.shard_map(
        local,
        mesh=mesh,
        in_specs=placed,
        out_specs=(P(("grp", "vec", "wlk"), None, None), P(("grp", "vec", "wlk"))),
        check_vma=False,
    )
```

```python
import functools
import math

import jax
import jax.numpy as jnp
from jax import lax
from jax.experimental import pallas as pl
from jax.experimental.pallas import tpu as pltpu
from jax.sharding import PartitionSpec as P

NS_ITERS = 2
EXTRA = 16

gradient_step = 0.25
energy_step = 0.002
epsilon = 1e-06

VMEM_LIMIT = 32 * 1024 * 1024


def call(body, out_shape, in_specs, out_specs, scratch=(), cost=None):
    return pl.pallas_call(
        body,
        out_shape=out_shape,
        in_specs=in_specs,
        out_specs=out_specs,
        scratch_shapes=list(scratch),
        cost_estimate=cost,
        compiler_params=pltpu.CompilerParams(vmem_limit_bytes=VMEM_LIMIT),
    )


def vmem(count):
    return [pl.BlockSpec(memory_space=pltpu.VMEM)] * count


def swap(array, axis, partner):
    size = lax.axis_size(axis)
    return lax.ppermute(array, axis, [(i, partner(i)) for i in range(size)])


def half_kernel(chol_ref, mine_ref, pair_ref):
    half, pair = mine_ref.shape[0], pair_ref.shape[0]
    here = lax.axis_index("wlk")
    first = lax.rem(here // 2, 2) * half
    mine_ref[...] = chol_ref[pl.ds(first, half)]
    pair_ref[...] = chol_ref[pl.ds(first + lax.rem(here, 2) * (half - pair), pair)]


def tile_kernel(log_ref, parent_ref, out_ref):
    rows = lax.broadcasted_iota(jnp.int32, out_ref.shape, 0)
    value = jnp.full(out_ref.shape, log_ref[0])
    high = value.astype(jnp.bfloat16).astype(jnp.float32)
    middle = (value - high).astype(jnp.bfloat16).astype(jnp.float32)
    low = value - high - middle
    parent = parent_ref[0].astype(jnp.float32)
    out_ref[...] = jnp.where(
        rows == 0, high, jnp.where(rows == 1, middle, jnp.where(rows == 2, low, parent))
    ).astype(jnp.bfloat16)


def payload_kernel(tile_ref, orbitals_ref, payload_ref):
    occupied = orbitals_ref.shape[1]
    payload_ref[:occupied, :] = orbitals_ref[0].astype(jnp.bfloat16)
    payload_ref[occupied:, :] = tile_ref[...]


def select_kernel(row_ref, theta_ref, extra_ref, other_ref):
    occupied, basis = theta_ref.shape
    here = lax.axis_index("wlk")

    def chosen(target, whole):
        extra = row_ref[target, occupied:, :].astype(jnp.float32)
        place = jnp.broadcast_to(extra[3:4, :], (whole, basis))
        picked = row_ref[0, :whole].astype(jnp.float32)
        for index in range(1, row_ref.shape[0]):
            picked = jnp.where(place == index, row_ref[index, :whole].astype(jnp.float32), picked)
        return picked.astype(jnp.bfloat16)

    own = chosen(here, row_ref.shape[1])
    theta_ref[...] = own[:occupied]
    extra_ref[...] = own[occupied:]
    other_ref[...] = chosen(jnp.bitwise_xor(here, 2), occupied)


def gradient_kernel(norm_scale, blocks, theta_ref, *refs):
    chol_refs, sum_refs = refs[:blocks], refs[blocks:-2]
    out_ref, adjoint = refs[-2:]
    occupied, basis = theta_ref.shape
    theta = theta_ref[...]
    rows = lax.broadcasted_iota(jnp.int32, (occupied, occupied), 0)
    columns = lax.broadcasted_iota(jnp.int32, (occupied, occupied), 1)
    diagonal = rows == columns
    turned = [
        lax.dot_general(
            ref[...].reshape(-1, basis), theta, (((1,), (1,)), ((), ())),
            preferred_element_type=jnp.float32,
        )
        for ref in chol_refs
    ]
    place = 0
    for product in turned:
        product = product.astype(jnp.bfloat16).astype(jnp.float32)
        for g in range(product.shape[0] // occupied):
            block = product[g * occupied : (g + 1) * occupied, :]
            on_diagonal = jnp.where(diagonal, block, 0.0)
            trace = jnp.sum(jnp.sum(on_diagonal, axis=0, keepdims=True), axis=1, keepdims=True)
            piece = norm_scale * (jnp.where(diagonal, trace, 0.0) - block)
            adjoint[:, place : place + occupied] = piece.astype(jnp.bfloat16)
            place += occupied
    total = sum_refs[0][...] if sum_refs else None
    place = 0
    for ref in chol_refs:
        width = ref.shape[0] * occupied
        term = jnp.dot(
            adjoint[:, place : place + width], ref[...].reshape(-1, basis),
            preferred_element_type=jnp.float32,
        )
        total = term if total is None else total + term
        place += width
    out_ref[...] = total.astype(out_ref.dtype)


def partial_gradient(norm_scale, theta, chols, dtype, *summand):
    occupied, basis = theta.shape
    width = sum(c.shape[0] for c in chols) * occupied
    return call(
        functools.partial(gradient_kernel, norm_scale, len(chols)),
        jax.ShapeDtypeStruct((occupied, basis), dtype),
        vmem(1 + len(chols) + len(summand)),
        pl.BlockSpec(memory_space=pltpu.VMEM),
        [pltpu.VMEM((occupied, width), jnp.bfloat16)],
    )(theta, *chols, *summand)


def final_kernel(theta_ref, extra_ref, own_ref, other_ref, propagator_ref, out_ref, log_ref):
    occupied, basis = theta_ref.shape
    theta = theta_ref[...].astype(jnp.float32)
    gradient = own_ref[...] + other_ref[...].astype(jnp.float32)
    energy = 0.5 * jnp.sum(theta * gradient)
    log_weight = jnp.sum(extra_ref[:3, :1].astype(jnp.float32))
    log_ref[0] = log_weight - energy_step * energy
    stepped = (theta - gradient_step * gradient).astype(jnp.bfloat16)
    propagated = jnp.dot(stepped, propagator_ref[...], preferred_element_type=jnp.float32)
    narrow = propagated.astype(jnp.bfloat16)
    overlap = lax.dot_general(
        narrow, narrow, (((1,), (1,)), ((), ())), preferred_element_type=jnp.float32
    )
    diagonal = lax.broadcasted_iota(jnp.int32, overlap.shape, 0) == lax.broadcasted_iota(
        jnp.int32, overlap.shape, 1
    )
    squares = jnp.sum(jnp.where(diagonal, overlap, 0.0), keepdims=True)
    scale = lax.rsqrt(squares / (occupied * basis) + epsilon)
    overlap = overlap * scale * (scale * (0.5 / basis))
    current = propagated * scale
    for index in range(NS_ITERS):
        if index:
            narrow = current.astype(jnp.bfloat16)
            overlap = lax.dot_general(
                narrow, narrow, (((1,), (1,)), ((), ())), preferred_element_type=jnp.float32
            ) * (0.5 / basis)
        else:
            narrow = current.astype(jnp.bfloat16)
        current = 1.5 * current - jnp.dot(
            overlap.astype(jnp.bfloat16), narrow, preferred_element_type=jnp.float32
        )
    out_ref[...] = current


def local(cholesky, orbitals, log_weights, parents, propagator):
    walker_count, occupied, basis = orbitals.shape
    vectors_here = cholesky.shape[0]
    vec_size, wlk_size = lax.axis_size("vec"), lax.axis_size("wlk")
    norm_scale = 1.0 / math.sqrt(vectors_here * vec_size)
    half = vectors_here // 2
    pair = (half + 1) // 2
    smem = pl.BlockSpec(memory_space=pltpu.SMEM)

    mine, part = call(
        half_kernel,
        (
            jax.ShapeDtypeStruct((half, occupied, basis), cholesky.dtype),
            jax.ShapeDtypeStruct((pair, occupied, basis), cholesky.dtype),
        ),
        vmem(1),
        vmem(2),
    )(cholesky)
    far = [
        lax.ppermute(
            mine,
            ("vec", "wlk"),
            [
                ((v ^ (2 * m + k % 2)) * wlk_size + k, v * wlk_size + k)
                for v in range(vec_size)
                for k in range(wlk_size)
            ],
        )
        for m in range(1, vec_size // 2)
    ]
    near = swap(part, "vec", lambda i: i ^ 1)

    tile = call(
        tile_kernel,
        jax.ShapeDtypeStruct((EXTRA, basis), jnp.bfloat16),
        [smem] * 2,
        vmem(1)[0],
    )(log_weights, parents)
    payload = call(
        payload_kernel,
        jax.ShapeDtypeStruct((occupied + EXTRA, basis), jnp.bfloat16),
        vmem(2),
        vmem(1)[0],
    )(tile, orbitals)
    row = lax.all_gather(payload, "wlk", axis=0)
    chosen, chosen_extra, neighbour = call(
        select_kernel,
        (
            jax.ShapeDtypeStruct((occupied, basis), jnp.bfloat16),
            jax.ShapeDtypeStruct((EXTRA, basis), jnp.bfloat16),
            jax.ShapeDtypeStruct((occupied, basis), jnp.bfloat16),
        ),
        vmem(1),
        vmem(3),
    )(row)

    *far, near, chosen = lax.optimization_barrier((*far, near, chosen))
    lacking = half - pair
    sent = lax.dynamic_slice_in_dim(near, lax.axis_index("wlk") % 2 * (pair - lacking), lacking, 0)
    vectors = [mine, near, *far]
    other = [swap(c, "wlk", lambda i: i ^ 1) for c in (sent, *far)]
    to_send = partial_gradient(norm_scale, neighbour, vectors, jnp.float32)
    to_send = partial_gradient(norm_scale, neighbour, other, jnp.bfloat16, to_send)
    received = swap(to_send, "wlk", lambda i: i ^ 2)
    own_part = partial_gradient(norm_scale, chosen, [*vectors, *other], jnp.float32)

    new_orbitals, new_logs = call(
        final_kernel,
        (
            jax.ShapeDtypeStruct((occupied, basis), jnp.float32),
            jax.ShapeDtypeStruct((1,), jnp.float32),
        ),
        vmem(5),
        [pl.BlockSpec(memory_space=pltpu.VMEM), smem],
    )(chosen, chosen_extra, own_part, received, propagator.T.astype(jnp.bfloat16))
    return new_orbitals.reshape(orbitals.shape), new_logs


def solution(mesh):
    placed = (
        P(("grp", "vec"), None, None),
        P(("grp", "vec", "wlk"), None, None),
        P(("grp", "vec", "wlk")),
        P(("grp", "vec", "wlk")),
        P("grp", None),
    )
    return jax.shard_map(
        local,
        mesh=mesh,
        in_specs=placed,
        out_specs=(P(("grp", "vec", "wlk"), None, None), P(("grp", "vec", "wlk"))),
        check_vma=False,
    )
```

```python
import functools
import math

import jax
import jax.numpy as jnp
from jax import lax
from jax.experimental import pallas as pl
from jax.experimental.pallas import tpu as pltpu
from jax.sharding import PartitionSpec as P

NS_ITERS = 2
EXTRA = 16

gradient_step = 0.25
energy_step = 0.002
epsilon = 1e-06

VMEM_LIMIT = 32 * 1024 * 1024


def call(body, out_shape, in_specs, out_specs, scratch=(), cost=None):
    return pl.pallas_call(
        body,
        out_shape=out_shape,
        in_specs=in_specs,
        out_specs=out_specs,
        scratch_shapes=list(scratch),
        cost_estimate=cost,
        compiler_params=pltpu.CompilerParams(vmem_limit_bytes=VMEM_LIMIT),
    )


def vmem(count):
    return [pl.BlockSpec(memory_space=pltpu.VMEM)] * count


def swap(array, axis, partner):
    size = lax.axis_size(axis)
    return lax.ppermute(array, axis, [(i, partner(i)) for i in range(size)])


def half_kernel(parent_ref, chol_ref, mine_ref, pair_ref):
    half, pair = mine_ref.shape[0], pair_ref.shape[0]
    here = lax.axis_index("wlk")
    first = lax.rem(here // 2, 2) * half
    mine_ref[...] = chol_ref[pl.ds(first, half)]
    pair_ref[...] = chol_ref[pl.ds(first + lax.rem(here, 2) * (half - pair), pair)]


def blank_kernel(out_ref):
    out_ref[...] = jnp.zeros(out_ref.shape, out_ref.dtype)


def parent_kernel(parent_ref, blank_ref, out_ref):
    out_ref[...] = blank_ref[...] + parent_ref[0].astype(jnp.float32)


def payload_kernel(log_ref, parent_ref, orbitals_ref, payload_ref):
    occupied, basis = orbitals_ref.shape[1:]
    payload_ref[:occupied, :] = orbitals_ref[0].astype(jnp.bfloat16)
    rows = lax.broadcasted_iota(jnp.int32, (EXTRA, basis), 0)
    value = jnp.full((EXTRA, basis), log_ref[0])
    high = value.astype(jnp.bfloat16).astype(jnp.float32)
    middle = (value - high).astype(jnp.bfloat16).astype(jnp.float32)
    low = value - high - middle
    parent = jnp.broadcast_to(parent_ref[:1, :1], value.shape)
    payload_ref[occupied:, :] = jnp.where(
        rows == 0, high, jnp.where(rows == 1, middle, jnp.where(rows == 2, low, parent))
    ).astype(jnp.bfloat16)


def select_kernel(row_ref, theta_ref, extra_ref, other_ref):
    occupied, basis = theta_ref.shape
    here = lax.axis_index("wlk")

    def chosen(target, whole):
        extra = row_ref[target, occupied:, :].astype(jnp.float32)
        place = jnp.broadcast_to(extra[3:4, :], (whole, basis))
        picked = row_ref[0, :whole].astype(jnp.float32)
        for index in range(1, row_ref.shape[0]):
            picked = jnp.where(place == index, row_ref[index, :whole].astype(jnp.float32), picked)
        return picked.astype(jnp.bfloat16)

    own = chosen(here, row_ref.shape[1])
    theta_ref[...] = own[:occupied]
    extra_ref[...] = own[occupied:]
    other_ref[...] = chosen(jnp.bitwise_xor(here, 2), occupied)


def gradient_kernel(norm_scale, blocks, theta_ref, *refs):
    chol_refs, sum_refs = refs[:blocks], refs[blocks:-2]
    out_ref, adjoint = refs[-2:]
    occupied, basis = theta_ref.shape
    theta = theta_ref[...]
    rows = lax.broadcasted_iota(jnp.int32, (occupied, occupied), 0)
    columns = lax.broadcasted_iota(jnp.int32, (occupied, occupied), 1)
    diagonal = rows == columns
    chol = jnp.concatenate([ref[...].reshape(-1, basis) for ref in chol_refs], axis=0)
    turned = lax.dot_general(
        chol, theta, (((1,), (1,)), ((), ())), preferred_element_type=jnp.float32
    )
    turned = turned.astype(jnp.bfloat16).astype(jnp.float32)
    for place in range(0, chol.shape[0], occupied):
        block = turned[place : place + occupied, :]
        on_diagonal = jnp.where(diagonal, block, 0.0)
        trace = jnp.sum(jnp.sum(on_diagonal, axis=0, keepdims=True), axis=1, keepdims=True)
        piece = norm_scale * (jnp.where(diagonal, trace, 0.0) - block)
        adjoint[:, place : place + occupied] = piece.astype(jnp.bfloat16)
    total = jnp.dot(adjoint[...], chol, preferred_element_type=jnp.float32)
    if sum_refs:
        total = total + sum_refs[0][...]
    out_ref[...] = total.astype(out_ref.dtype)


def partial_gradient(norm_scale, theta, chols, dtype, *summand):
    occupied, basis = theta.shape
    width = sum(c.shape[0] for c in chols) * occupied
    return call(
        functools.partial(gradient_kernel, norm_scale, len(chols)),
        jax.ShapeDtypeStruct((occupied, basis), dtype),
        vmem(1 + len(chols) + len(summand)),
        pl.BlockSpec(memory_space=pltpu.VMEM),
        [pltpu.VMEM((occupied, width), jnp.bfloat16)],
    )(theta, *chols, *summand)


def final_kernel(theta_ref, extra_ref, own_ref, other_ref, propagator_ref, out_ref, log_ref):
    occupied, basis = theta_ref.shape
    theta = theta_ref[...].astype(jnp.float32)
    gradient = own_ref[...] + other_ref[...].astype(jnp.float32)
    energy = 0.5 * jnp.sum(theta * gradient)
    log_weight = jnp.sum(extra_ref[:3, :1].astype(jnp.float32))
    log_ref[0] = log_weight - energy_step * energy
    stepped = (theta - gradient_step * gradient).astype(jnp.bfloat16)
    propagated = jnp.dot(stepped, propagator_ref[...], preferred_element_type=jnp.float32)
    narrow = propagated.astype(jnp.bfloat16)
    overlap = lax.dot_general(
        narrow, narrow, (((1,), (1,)), ((), ())), preferred_element_type=jnp.float32
    )
    diagonal = lax.broadcasted_iota(jnp.int32, overlap.shape, 0) == lax.broadcasted_iota(
        jnp.int32, overlap.shape, 1
    )
    squares = jnp.sum(jnp.where(diagonal, overlap, 0.0), keepdims=True)
    scale = lax.rsqrt(squares / (occupied * basis) + epsilon)
    overlap = overlap * scale * (scale * (0.5 / basis))
    current = propagated * scale
    for index in range(NS_ITERS):
        if index:
            narrow = current.astype(jnp.bfloat16)
            overlap = lax.dot_general(
                narrow, narrow, (((1,), (1,)), ((), ())), preferred_element_type=jnp.float32
            ) * (0.5 / basis)
        else:
            narrow = current.astype(jnp.bfloat16)
        current = 1.5 * current - jnp.dot(
            overlap.astype(jnp.bfloat16), narrow, preferred_element_type=jnp.float32
        )
    out_ref[...] = current


def local(cholesky, orbitals, log_weights, parents, propagator):
    walker_count, occupied, basis = orbitals.shape
    vectors_here = cholesky.shape[0]
    vec_size, wlk_size = lax.axis_size("vec"), lax.axis_size("wlk")
    norm_scale = 1.0 / math.sqrt(vectors_here * vec_size)
    half = vectors_here // 2
    pair = (half + 1) // 2
    smem = pl.BlockSpec(memory_space=pltpu.SMEM)

    blank = call(
        blank_kernel,
        jax.ShapeDtypeStruct((8, 128), jnp.float32),
        [],
        vmem(1)[0],
        (),
        pl.CostEstimate(flops=10**11, bytes_accessed=256 * 2**20, transcendentals=0),
    )()
    parent = call(
        parent_kernel,
        jax.ShapeDtypeStruct((8, 128), jnp.float32),
        [smem] + vmem(1),
        vmem(1)[0],
    )(parents, blank)
    mine, part = call(
        half_kernel,
        (
            jax.ShapeDtypeStruct((half, occupied, basis), cholesky.dtype),
            jax.ShapeDtypeStruct((pair, occupied, basis), cholesky.dtype),
        ),
        vmem(2),
        vmem(2),
    )(parent, cholesky)
    far = [
        lax.ppermute(
            mine,
            ("vec", "wlk"),
            [
                ((v ^ (2 * m + k % 2)) * wlk_size + k, v * wlk_size + k)
                for v in range(vec_size)
                for k in range(wlk_size)
            ],
        )
        for m in range(1, vec_size // 2)
    ]
    near = swap(part, "vec", lambda i: i ^ 1)

    payload = call(
        payload_kernel,
        jax.ShapeDtypeStruct((occupied + EXTRA, basis), jnp.bfloat16),
        [smem] + vmem(2),
        vmem(1)[0],
    )(log_weights, parent, orbitals)
    row = lax.all_gather(payload, "wlk", axis=0)
    chosen, chosen_extra, neighbour = call(
        select_kernel,
        (
            jax.ShapeDtypeStruct((occupied, basis), jnp.bfloat16),
            jax.ShapeDtypeStruct((EXTRA, basis), jnp.bfloat16),
            jax.ShapeDtypeStruct((occupied, basis), jnp.bfloat16),
        ),
        vmem(1),
        vmem(3),
    )(row)

    *far, near, chosen = lax.optimization_barrier((*far, near, chosen))
    lacking = half - pair
    sent = lax.dynamic_slice_in_dim(near, lax.axis_index("wlk") % 2 * (pair - lacking), lacking, 0)
    vectors = [mine, near, *far]
    other = [swap(jnp.concatenate([sent, *far], axis=0), "wlk", lambda i: i ^ 1)]
    to_send = partial_gradient(norm_scale, neighbour, vectors, jnp.float32)
    to_send = partial_gradient(norm_scale, neighbour, other, jnp.bfloat16, to_send)
    received = swap(to_send, "wlk", lambda i: i ^ 2)
    own_part = partial_gradient(norm_scale, chosen, [*vectors, *other], jnp.float32)

    new_orbitals, new_logs = call(
        final_kernel,
        (
            jax.ShapeDtypeStruct((occupied, basis), jnp.float32),
            jax.ShapeDtypeStruct((1,), jnp.float32),
        ),
        vmem(5),
        [pl.BlockSpec(memory_space=pltpu.VMEM), smem],
    )(chosen, chosen_extra, own_part, received, propagator.T.astype(jnp.bfloat16))
    return new_orbitals.reshape(orbitals.shape), new_logs


def solution(mesh):
    placed = (
        P(("grp", "vec"), None, None),
        P(("grp", "vec", "wlk"), None, None),
        P(("grp", "vec", "wlk")),
        P(("grp", "vec", "wlk")),
        P("grp", None),
    )
    return jax.shard_map(
        local,
        mesh=mesh,
        in_specs=placed,
        out_specs=(P(("grp", "vec", "wlk"), None, None), P(("grp", "vec", "wlk"))),
        check_vma=False,
    )
```

```python
import functools
import math

import jax
import jax.numpy as jnp
from jax import lax
from jax.experimental import pallas as pl
from jax.experimental.pallas import tpu as pltpu
from jax.sharding import PartitionSpec as P

NS_ITERS = 2
EXTRA = 16

gradient_step = 0.25
energy_step = 0.002
epsilon = 1e-06

VMEM_LIMIT = 32 * 1024 * 1024


def call(body, out_shape, in_specs, out_specs, scratch=(), cost=None):
    return pl.pallas_call(
        body,
        out_shape=out_shape,
        in_specs=in_specs,
        out_specs=out_specs,
        scratch_shapes=list(scratch),
        cost_estimate=cost,
        compiler_params=pltpu.CompilerParams(vmem_limit_bytes=VMEM_LIMIT),
    )


def vmem(count):
    return [pl.BlockSpec(memory_space=pltpu.VMEM)] * count


def swap(array, axis, partner):
    size = lax.axis_size(axis)
    return lax.ppermute(array, axis, [(i, partner(i)) for i in range(size)])


def half_kernel(parent_ref, chol_ref, mine_ref, pair_ref):
    half, pair = mine_ref.shape[0], pair_ref.shape[0]
    here = lax.axis_index("wlk")
    first = lax.rem(here // 2, 2) * half
    mine_ref[...] = chol_ref[pl.ds(first, half)]
    pair_ref[...] = chol_ref[pl.ds(first + lax.rem(here, 2) * (half - pair), pair)]


def blank_kernel(out_ref):
    out_ref[...] = jnp.zeros(out_ref.shape, out_ref.dtype)


def parent_kernel(parent_ref, blank_ref, out_ref):
    out_ref[...] = blank_ref[...] + parent_ref[0].astype(jnp.float32)


def payload_kernel(log_ref, parent_ref, orbitals_ref, payload_ref):
    occupied, basis = orbitals_ref.shape[1:]
    payload_ref[:occupied, :] = orbitals_ref[0].astype(jnp.bfloat16)
    rows = lax.broadcasted_iota(jnp.int32, (EXTRA, basis), 0)
    value = jnp.full((EXTRA, basis), log_ref[0])
    high = value.astype(jnp.bfloat16).astype(jnp.float32)
    middle = (value - high).astype(jnp.bfloat16).astype(jnp.float32)
    low = value - high - middle
    parent = jnp.broadcast_to(parent_ref[:1, :1], value.shape)
    payload_ref[occupied:, :] = jnp.where(
        rows == 0, high, jnp.where(rows == 1, middle, jnp.where(rows == 2, low, parent))
    ).astype(jnp.bfloat16)


def select_kernel(row_ref, theta_ref, extra_ref, other_ref):
    occupied, basis = theta_ref.shape
    here = lax.axis_index("wlk")

    def chosen(target, whole):
        extra = row_ref[target, occupied:, :].astype(jnp.float32)
        place = jnp.broadcast_to(extra[3:4, :], (whole, basis))
        picked = row_ref[0, :whole].astype(jnp.float32)
        for index in range(1, row_ref.shape[0]):
            picked = jnp.where(place == index, row_ref[index, :whole].astype(jnp.float32), picked)
        return picked.astype(jnp.bfloat16)

    own = chosen(here, row_ref.shape[1])
    theta_ref[...] = own[:occupied]
    extra_ref[...] = own[occupied:]
    other_ref[...] = chosen(jnp.bitwise_xor(here, 2), occupied)


def gradient_kernel(norm_scale, blocks, theta_ref, *refs):
    chol_refs, sum_refs = refs[:blocks], refs[blocks:-2]
    out_ref, adjoint = refs[-2:]
    occupied, basis = theta_ref.shape
    theta = theta_ref[...]
    rows = lax.broadcasted_iota(jnp.int32, (occupied, occupied), 0)
    columns = lax.broadcasted_iota(jnp.int32, (occupied, occupied), 1)
    diagonal = rows == columns
    chol = jnp.concatenate([ref[...].reshape(-1, basis) for ref in chol_refs], axis=0)
    turned = lax.dot_general(
        chol, theta, (((1,), (1,)), ((), ())), preferred_element_type=jnp.float32
    )
    turned = turned.astype(jnp.bfloat16).astype(jnp.float32)
    for place in range(0, chol.shape[0], occupied):
        block = turned[place : place + occupied, :]
        on_diagonal = jnp.where(diagonal, block, 0.0)
        trace = jnp.sum(jnp.sum(on_diagonal, axis=0, keepdims=True), axis=1, keepdims=True)
        piece = norm_scale * (jnp.where(diagonal, trace, 0.0) - block)
        adjoint[:, place : place + occupied] = piece.astype(jnp.bfloat16)
    total = jnp.dot(adjoint[...], chol, preferred_element_type=jnp.float32)
    if sum_refs:
        total = total + sum_refs[0][...]
    out_ref[...] = total.astype(out_ref.dtype)


def partial_gradient(norm_scale, theta, chols, dtype, *summand):
    occupied, basis = theta.shape
    width = sum(c.shape[0] for c in chols) * occupied
    return call(
        functools.partial(gradient_kernel, norm_scale, len(chols)),
        jax.ShapeDtypeStruct((occupied, basis), dtype),
        vmem(1 + len(chols) + len(summand)),
        pl.BlockSpec(memory_space=pltpu.VMEM),
        [pltpu.VMEM((occupied, width), jnp.bfloat16)],
    )(theta, *chols, *summand)


def final_kernel(theta_ref, extra_ref, own_ref, other_ref, propagator_ref, out_ref, log_ref):
    occupied, basis = theta_ref.shape
    theta = theta_ref[...].astype(jnp.float32)
    gradient = own_ref[...] + other_ref[...].astype(jnp.float32)
    energy = 0.5 * jnp.sum(theta * gradient)
    log_weight = jnp.sum(extra_ref[...].astype(jnp.float32)[:3, :1])
    log_ref[0] = log_weight - energy_step * energy
    stepped = (theta - gradient_step * gradient).astype(jnp.bfloat16)
    propagated = jnp.dot(stepped, propagator_ref[...], preferred_element_type=jnp.float32)
    narrow = propagated.astype(jnp.bfloat16)
    overlap = lax.dot_general(
        narrow, narrow, (((1,), (1,)), ((), ())), preferred_element_type=jnp.float32
    )
    diagonal = lax.broadcasted_iota(jnp.int32, overlap.shape, 0) == lax.broadcasted_iota(
        jnp.int32, overlap.shape, 1
    )
    squares = jnp.sum(jnp.where(diagonal, overlap, 0.0), keepdims=True)
    scale = lax.rsqrt(squares / (occupied * basis) + epsilon)
    overlap = overlap * scale * (scale * (0.5 / basis))
    current = propagated * scale
    for index in range(NS_ITERS):
        if index:
            narrow = current.astype(jnp.bfloat16)
            overlap = lax.dot_general(
                narrow, narrow, (((1,), (1,)), ((), ())), preferred_element_type=jnp.float32
            ) * (0.5 / basis)
        else:
            narrow = current.astype(jnp.bfloat16)
        current = 1.5 * current - jnp.dot(
            overlap.astype(jnp.bfloat16), narrow, preferred_element_type=jnp.float32
        )
    out_ref[...] = current


def local(cholesky, orbitals, log_weights, parents, propagator):
    walker_count, occupied, basis = orbitals.shape
    vectors_here = cholesky.shape[0]
    vec_size, wlk_size = lax.axis_size("vec"), lax.axis_size("wlk")
    norm_scale = 1.0 / math.sqrt(vectors_here * vec_size)
    half = vectors_here // 2
    pair = (half + 1) // 2
    smem = pl.BlockSpec(memory_space=pltpu.SMEM)

    blank = call(
        blank_kernel,
        jax.ShapeDtypeStruct((8, 128), jnp.float32),
        [],
        vmem(1)[0],
        (),
        pl.CostEstimate(flops=10**11, bytes_accessed=256 * 2**20, transcendentals=0),
    )()
    parent = call(
        parent_kernel,
        jax.ShapeDtypeStruct((8, 128), jnp.float32),
        [smem] + vmem(1),
        vmem(1)[0],
    )(parents, blank)
    mine, part = call(
        half_kernel,
        (
            jax.ShapeDtypeStruct((half, occupied, basis), cholesky.dtype),
            jax.ShapeDtypeStruct((pair, occupied, basis), cholesky.dtype),
        ),
        vmem(2),
        vmem(2),
    )(parent, cholesky)
    far = [
        lax.ppermute(
            mine,
            ("vec", "wlk"),
            [
                ((v ^ (2 * m + k % 2)) * wlk_size + k, v * wlk_size + k)
                for v in range(vec_size)
                for k in range(wlk_size)
            ],
        )
        for m in range(1, vec_size // 2)
    ]
    near = swap(part, "vec", lambda i: i ^ 1)

    payload = call(
        payload_kernel,
        jax.ShapeDtypeStruct((occupied + EXTRA, basis), jnp.bfloat16),
        [smem] + vmem(2),
        vmem(1)[0],
    )(log_weights, parent, orbitals)
    row = lax.all_gather(payload, "wlk", axis=0)
    chosen, chosen_extra, neighbour = call(
        select_kernel,
        (
            jax.ShapeDtypeStruct((occupied, basis), jnp.bfloat16),
            jax.ShapeDtypeStruct((EXTRA, basis), jnp.bfloat16),
            jax.ShapeDtypeStruct((occupied, basis), jnp.bfloat16),
        ),
        vmem(1),
        vmem(3),
    )(row)

    *far, near, chosen = lax.optimization_barrier((*far, near, chosen))
    lacking = half - pair
    sent = lax.dynamic_slice_in_dim(near, lax.axis_index("wlk") % 2 * (pair - lacking), lacking, 0)
    vectors = [mine, near, *far]
    other = [swap(jnp.concatenate([sent, *far], axis=0), "wlk", lambda i: i ^ 1)]
    to_send = partial_gradient(norm_scale, neighbour, vectors, jnp.float32)
    to_send = partial_gradient(norm_scale, neighbour, other, jnp.bfloat16, to_send)
    received = swap(to_send, "wlk", lambda i: i ^ 2)
    own_part = partial_gradient(norm_scale, chosen, [*vectors, *other], jnp.float32)

    new_orbitals, new_logs = call(
        final_kernel,
        (
            jax.ShapeDtypeStruct((occupied, basis), jnp.float32),
            jax.ShapeDtypeStruct((1,), jnp.float32),
        ),
        vmem(5),
        [pl.BlockSpec(memory_space=pltpu.VMEM), smem],
    )(chosen, chosen_extra, own_part, received, propagator.T.astype(jnp.bfloat16))
    return new_orbitals.reshape(orbitals.shape), new_logs


def solution(mesh):
    placed = (
        P(("grp", "vec"), None, None),
        P(("grp", "vec", "wlk"), None, None),
        P(("grp", "vec", "wlk")),
        P(("grp", "vec", "wlk")),
        P("grp", None),
    )
    return jax.shard_map(
        local,
        mesh=mesh,
        in_specs=placed,
        out_specs=(P(("grp", "vec", "wlk"), None, None), P(("grp", "vec", "wlk"))),
        check_vma=False,
    )
```

```python
import functools
import math

import jax
import jax.numpy as jnp
from jax import lax
from jax.experimental import pallas as pl
from jax.experimental.pallas import tpu as pltpu
from jax.sharding import PartitionSpec as P

NS_ITERS = 2
EXTRA = 16

gradient_step = 0.25
energy_step = 0.002
epsilon = 1e-06

VMEM_LIMIT = 32 * 1024 * 1024


def call(body, out_shape, in_specs, out_specs, scratch=(), cost=None):
    return pl.pallas_call(
        body,
        out_shape=out_shape,
        in_specs=in_specs,
        out_specs=out_specs,
        scratch_shapes=list(scratch),
        cost_estimate=cost,
        compiler_params=pltpu.CompilerParams(vmem_limit_bytes=VMEM_LIMIT),
    )


def vmem(count):
    return [pl.BlockSpec(memory_space=pltpu.VMEM)] * count


def swap(array, axis, partner):
    size = lax.axis_size(axis)
    return lax.ppermute(array, axis, [(i, partner(i)) for i in range(size)])


def half_kernel(parent_ref, chol_ref, mine_ref, pair_ref):
    half, pair = mine_ref.shape[0], pair_ref.shape[0]
    here = lax.axis_index("wlk")
    first = lax.rem(here // 2, 2) * half
    mine_ref[...] = chol_ref[pl.ds(first, half)]
    pair_ref[...] = chol_ref[pl.ds(first + lax.rem(here, 2) * (half - pair), pair)]


def blank_kernel(out_ref):
    out_ref[...] = jnp.zeros(out_ref.shape, out_ref.dtype)


def parent_kernel(parent_ref, blank_ref, out_ref):
    out_ref[...] = blank_ref[...] + parent_ref[0].astype(jnp.float32)


def payload_kernel(log_ref, parent_ref, orbitals_ref, payload_ref):
    occupied, basis = orbitals_ref.shape[1:]
    payload_ref[:occupied, :] = orbitals_ref[0].astype(jnp.bfloat16)
    rows = lax.broadcasted_iota(jnp.int32, (EXTRA, basis), 0)
    value = jnp.full((EXTRA, basis), log_ref[0])
    high = value.astype(jnp.bfloat16).astype(jnp.float32)
    middle = (value - high).astype(jnp.bfloat16).astype(jnp.float32)
    low = value - high - middle
    parent = jnp.broadcast_to(parent_ref[:1, :1], value.shape)
    payload_ref[occupied:, :] = jnp.where(
        rows == 0, high, jnp.where(rows == 1, middle, jnp.where(rows == 2, low, parent))
    ).astype(jnp.bfloat16)


def select_kernel(row_ref, theta_ref, extra_ref, other_ref):
    occupied, basis = theta_ref.shape
    here = lax.axis_index("wlk")

    def chosen(target, whole):
        extra = row_ref[target, occupied:, :].astype(jnp.float32)
        place = jnp.broadcast_to(extra[3:4, :], (whole, basis))
        picked = row_ref[0, :whole].astype(jnp.float32)
        for index in range(1, row_ref.shape[0]):
            picked = jnp.where(place == index, row_ref[index, :whole].astype(jnp.float32), picked)
        return picked.astype(jnp.bfloat16)

    own = chosen(here, row_ref.shape[1])
    theta_ref[...] = own[:occupied]
    extra_ref[...] = own[occupied:]
    other_ref[...] = chosen(jnp.bitwise_xor(here, 2), occupied)


def gradient_kernel(norm_scale, blocks, theta_ref, *refs):
    chol_refs, sum_refs = refs[:blocks], refs[blocks:-2]
    out_ref, adjoint = refs[-2:]
    occupied, basis = theta_ref.shape
    theta = theta_ref[...]
    rows = lax.broadcasted_iota(jnp.int32, (occupied, occupied), 0)
    columns = lax.broadcasted_iota(jnp.int32, (occupied, occupied), 1)
    diagonal = rows == columns
    chol = jnp.concatenate([ref[...].reshape(-1, basis) for ref in chol_refs], axis=0)
    turned = lax.dot_general(
        chol, theta, (((1,), (1,)), ((), ())), preferred_element_type=jnp.float32
    )
    turned = turned.astype(jnp.bfloat16).astype(jnp.float32)
    for place in range(0, chol.shape[0], occupied):
        block = turned[place : place + occupied, :]
        on_diagonal = jnp.where(diagonal, block, 0.0)
        trace = jnp.sum(jnp.sum(on_diagonal, axis=0, keepdims=True), axis=1, keepdims=True)
        piece = norm_scale * (jnp.where(diagonal, trace, 0.0) - block)
        adjoint[:, place : place + occupied] = piece.astype(jnp.bfloat16)
    total = jnp.dot(adjoint[...], chol, preferred_element_type=jnp.float32)
    if sum_refs:
        total = total + sum_refs[0][...]
    out_ref[...] = total.astype(out_ref.dtype)


def partial_gradient(norm_scale, theta, chols, dtype, *summand):
    occupied, basis = theta.shape
    width = sum(c.shape[0] for c in chols) * occupied
    return call(
        functools.partial(gradient_kernel, norm_scale, len(chols)),
        jax.ShapeDtypeStruct((occupied, basis), dtype),
        vmem(1 + len(chols) + len(summand)),
        pl.BlockSpec(memory_space=pltpu.VMEM),
        [pltpu.VMEM((occupied, width), jnp.bfloat16)],
    )(theta, *chols, *summand)


def final_kernel(theta_ref, extra_ref, own_ref, other_ref, propagator_ref, out_ref, log_ref):
    occupied, basis = theta_ref.shape
    theta = theta_ref[...].astype(jnp.float32)
    gradient = own_ref[...] + other_ref[...].astype(jnp.float32)
    energy = 0.5 * jnp.sum(theta * gradient)
    log_weight = jnp.sum(extra_ref[...].astype(jnp.float32)[:3, :1])
    log_ref[0] = log_weight - energy_step * energy
    stepped = (theta - gradient_step * gradient).astype(jnp.bfloat16)
    propagated = jnp.dot(stepped, propagator_ref[...], preferred_element_type=jnp.float32)
    narrow = propagated.astype(jnp.bfloat16)
    overlap = lax.dot_general(
        narrow, narrow, (((1,), (1,)), ((), ())), preferred_element_type=jnp.float32
    )
    diagonal = lax.broadcasted_iota(jnp.int32, overlap.shape, 0) == lax.broadcasted_iota(
        jnp.int32, overlap.shape, 1
    )
    squares = jnp.sum(jnp.where(diagonal, overlap, 0.0), keepdims=True)
    scale = lax.rsqrt(squares / (occupied * basis) + epsilon)
    overlap = overlap * scale * (scale * (0.5 / basis))
    current = propagated * scale
    for index in range(NS_ITERS):
        if index:
            narrow = current.astype(jnp.bfloat16)
            overlap = lax.dot_general(
                narrow, narrow, (((1,), (1,)), ((), ())), preferred_element_type=jnp.float32
            ) * (0.5 / basis)
        else:
            narrow = current.astype(jnp.bfloat16)
        current = 1.5 * current - jnp.dot(
            overlap.astype(jnp.bfloat16), narrow, preferred_element_type=jnp.float32
        )
    out_ref[...] = current


def local(cholesky, orbitals, log_weights, parents, propagator):
    walker_count, occupied, basis = orbitals.shape
    vectors_here = cholesky.shape[0]
    vec_size, wlk_size = lax.axis_size("vec"), lax.axis_size("wlk")
    norm_scale = 1.0 / math.sqrt(vectors_here * vec_size)
    half = vectors_here // 2
    pair = (half + 1) // 2
    smem = pl.BlockSpec(memory_space=pltpu.SMEM)

    blank = call(
        blank_kernel,
        jax.ShapeDtypeStruct((8, 128), jnp.float32),
        [],
        vmem(1)[0],
        (),
        pl.CostEstimate(flops=10**11, bytes_accessed=256 * 2**20, transcendentals=0),
    )()
    parent = call(
        parent_kernel,
        jax.ShapeDtypeStruct((8, 128), jnp.float32),
        [smem] + vmem(1),
        vmem(1)[0],
    )(parents, blank)
    mine, part = call(
        half_kernel,
        (
            jax.ShapeDtypeStruct((half, occupied, basis), cholesky.dtype),
            jax.ShapeDtypeStruct((pair, occupied, basis), cholesky.dtype),
        ),
        vmem(2),
        vmem(2),
    )(parent, cholesky)
    far = [
        lax.ppermute(
            mine,
            ("vec", "wlk"),
            [
                ((v ^ (2 * m + 1 - k % 2)) * wlk_size + k, v * wlk_size + k)
                for v in range(vec_size)
                for k in range(wlk_size)
            ],
        )
        for m in range(1, vec_size // 2)
    ]
    near = swap(part, "vec", lambda i: i ^ 1)

    payload = call(
        payload_kernel,
        jax.ShapeDtypeStruct((occupied + EXTRA, basis), jnp.bfloat16),
        [smem] + vmem(2),
        vmem(1)[0],
    )(log_weights, parent, orbitals)
    row = lax.all_gather(payload, "wlk", axis=0)
    chosen, chosen_extra, neighbour = call(
        select_kernel,
        (
            jax.ShapeDtypeStruct((occupied, basis), jnp.bfloat16),
            jax.ShapeDtypeStruct((EXTRA, basis), jnp.bfloat16),
            jax.ShapeDtypeStruct((occupied, basis), jnp.bfloat16),
        ),
        vmem(1),
        vmem(3),
    )(row)

    *far, near, chosen = lax.optimization_barrier((*far, near, chosen))
    lacking = half - pair
    sent = lax.dynamic_slice_in_dim(near, lax.axis_index("wlk") % 2 * (pair - lacking), lacking, 0)
    vectors = [mine, near, *far]
    other = [swap(jnp.concatenate([sent, *far], axis=0), "wlk", lambda i: i ^ 1)]
    to_send = partial_gradient(norm_scale, neighbour, vectors, jnp.float32)
    to_send = partial_gradient(norm_scale, neighbour, other, jnp.bfloat16, to_send)
    received = swap(to_send, "wlk", lambda i: i ^ 2)
    own_part = partial_gradient(norm_scale, chosen, [*vectors, *other], jnp.float32)

    new_orbitals, new_logs = call(
        final_kernel,
        (
            jax.ShapeDtypeStruct((occupied, basis), jnp.float32),
            jax.ShapeDtypeStruct((1,), jnp.float32),
        ),
        vmem(5),
        [pl.BlockSpec(memory_space=pltpu.VMEM), smem],
    )(chosen, chosen_extra, own_part, received, propagator.T.astype(jnp.bfloat16))
    return new_orbitals.reshape(orbitals.shape), new_logs


def solution(mesh):
    placed = (
        P(("grp", "vec"), None, None),
        P(("grp", "vec", "wlk"), None, None),
        P(("grp", "vec", "wlk")),
        P(("grp", "vec", "wlk")),
        P("grp", None),
    )
    return jax.shard_map(
        local,
        mesh=mesh,
        in_specs=placed,
        out_specs=(P(("grp", "vec", "wlk"), None, None), P(("grp", "vec", "wlk"))),
        check_vma=False,
    )
```

```python
import functools
import math

import jax
import jax.numpy as jnp
from jax import lax
from jax.experimental import pallas as pl
from jax.experimental.pallas import tpu as pltpu
from jax.sharding import PartitionSpec as P

NS_ITERS = 2
EXTRA = 16

gradient_step = 0.25
energy_step = 0.002
epsilon = 1e-06

VMEM_LIMIT = 32 * 1024 * 1024


def call(body, out_shape, in_specs, out_specs, scratch=(), cost=None):
    return pl.pallas_call(
        body,
        out_shape=out_shape,
        in_specs=in_specs,
        out_specs=out_specs,
        scratch_shapes=list(scratch),
        cost_estimate=cost,
        compiler_params=pltpu.CompilerParams(vmem_limit_bytes=VMEM_LIMIT),
    )


def vmem(count):
    return [pl.BlockSpec(memory_space=pltpu.VMEM)] * count


def swap(array, axis, partner):
    size = lax.axis_size(axis)
    return lax.ppermute(array, axis, [(i, partner(i)) for i in range(size)])


def half_kernel(parent_ref, chol_ref, mine_ref, pair_ref):
    half, pair = mine_ref.shape[0], pair_ref.shape[0]
    here = lax.axis_index("wlk")
    first = lax.rem(here // 2, 2) * half
    mine_ref[...] = chol_ref[pl.ds(first, half)]
    pair_ref[...] = chol_ref[pl.ds(first + lax.rem(here, 2) * (half - pair), pair)]


def blank_kernel(out_ref):
    out_ref[...] = jnp.zeros(out_ref.shape, out_ref.dtype)


def parent_kernel(parent_ref, blank_ref, out_ref):
    out_ref[...] = blank_ref[...] + parent_ref[0].astype(jnp.float32)


def payload_kernel(log_ref, parent_ref, orbitals_ref, payload_ref):
    occupied, basis = orbitals_ref.shape[1:]
    payload_ref[:occupied, :] = orbitals_ref[0].astype(jnp.bfloat16)
    rows = lax.broadcasted_iota(jnp.int32, (EXTRA, basis), 0)
    value = jnp.full((EXTRA, basis), log_ref[0])
    high = value.astype(jnp.bfloat16).astype(jnp.float32)
    middle = (value - high).astype(jnp.bfloat16).astype(jnp.float32)
    low = value - high - middle
    parent = jnp.broadcast_to(parent_ref[:1, :1], value.shape)
    payload_ref[occupied:, :] = jnp.where(
        rows == 0, high, jnp.where(rows == 1, middle, jnp.where(rows == 2, low, parent))
    ).astype(jnp.bfloat16)


def select_kernel(row_ref, theta_ref, extra_ref, other_ref):
    occupied, basis = theta_ref.shape
    here = lax.axis_index("wlk")

    def chosen(target, whole):
        extra = row_ref[target, occupied:, :].astype(jnp.float32)
        place = jnp.broadcast_to(extra[3:4, :], (whole, basis))
        picked = row_ref[0, :whole].astype(jnp.float32)
        for index in range(1, row_ref.shape[0]):
            picked = jnp.where(place == index, row_ref[index, :whole].astype(jnp.float32), picked)
        return picked.astype(jnp.bfloat16)

    own = chosen(here, row_ref.shape[1])
    theta_ref[...] = own[:occupied]
    extra_ref[...] = own[occupied:]
    other_ref[...] = chosen(jnp.bitwise_xor(here, 3), occupied)


def gradient_kernel(norm_scale, blocks, theta_ref, *refs):
    chol_refs, sum_refs = refs[:blocks], refs[blocks:-2]
    out_ref, adjoint = refs[-2:]
    occupied, basis = theta_ref.shape
    theta = theta_ref[...]
    rows = lax.broadcasted_iota(jnp.int32, (occupied, occupied), 0)
    columns = lax.broadcasted_iota(jnp.int32, (occupied, occupied), 1)
    diagonal = rows == columns
    chol = jnp.concatenate([ref[...].reshape(-1, basis) for ref in chol_refs], axis=0)
    turned = lax.dot_general(
        chol, theta, (((1,), (1,)), ((), ())), preferred_element_type=jnp.float32
    )
    turned = turned.astype(jnp.bfloat16).astype(jnp.float32)
    for place in range(0, chol.shape[0], occupied):
        block = turned[place : place + occupied, :]
        on_diagonal = jnp.where(diagonal, block, 0.0)
        trace = jnp.sum(jnp.sum(on_diagonal, axis=0, keepdims=True), axis=1, keepdims=True)
        piece = norm_scale * (jnp.where(diagonal, trace, 0.0) - block)
        adjoint[:, place : place + occupied] = piece.astype(jnp.bfloat16)
    total = jnp.dot(adjoint[...], chol, preferred_element_type=jnp.float32)
    if sum_refs:
        total = total + sum_refs[0][...]
    out_ref[...] = total.astype(out_ref.dtype)


def partial_gradient(norm_scale, theta, chols, dtype, *summand):
    occupied, basis = theta.shape
    width = sum(c.shape[0] for c in chols) * occupied
    return call(
        functools.partial(gradient_kernel, norm_scale, len(chols)),
        jax.ShapeDtypeStruct((occupied, basis), dtype),
        vmem(1 + len(chols) + len(summand)),
        pl.BlockSpec(memory_space=pltpu.VMEM),
        [pltpu.VMEM((occupied, width), jnp.bfloat16)],
    )(theta, *chols, *summand)


def final_kernel(theta_ref, extra_ref, own_ref, other_ref, propagator_ref, out_ref, log_ref):
    occupied, basis = theta_ref.shape
    theta = theta_ref[...].astype(jnp.float32)
    gradient = own_ref[...] + other_ref[...].astype(jnp.float32)
    energy = 0.5 * jnp.sum(theta * gradient)
    log_weight = jnp.sum(extra_ref[...].astype(jnp.float32)[:3, :1])
    log_ref[0] = log_weight - energy_step * energy
    stepped = (theta - gradient_step * gradient).astype(jnp.bfloat16)
    propagated = jnp.dot(stepped, propagator_ref[...], preferred_element_type=jnp.float32)
    narrow = propagated.astype(jnp.bfloat16)
    overlap = lax.dot_general(
        narrow, narrow, (((1,), (1,)), ((), ())), preferred_element_type=jnp.float32
    )
    diagonal = lax.broadcasted_iota(jnp.int32, overlap.shape, 0) == lax.broadcasted_iota(
        jnp.int32, overlap.shape, 1
    )
    squares = jnp.sum(jnp.where(diagonal, overlap, 0.0), keepdims=True)
    scale = lax.rsqrt(squares / (occupied * basis) + epsilon)
    overlap = overlap * scale * (scale * (0.5 / basis))
    current = propagated * scale
    for index in range(NS_ITERS):
        if index:
            narrow = current.astype(jnp.bfloat16)
            overlap = lax.dot_general(
                narrow, narrow, (((1,), (1,)), ((), ())), preferred_element_type=jnp.float32
            ) * (0.5 / basis)
        else:
            narrow = current.astype(jnp.bfloat16)
        current = 1.5 * current - jnp.dot(
            overlap.astype(jnp.bfloat16), narrow, preferred_element_type=jnp.float32
        )
    out_ref[...] = current


def local(cholesky, orbitals, log_weights, parents, propagator):
    walker_count, occupied, basis = orbitals.shape
    vectors_here = cholesky.shape[0]
    vec_size, wlk_size = lax.axis_size("vec"), lax.axis_size("wlk")
    norm_scale = 1.0 / math.sqrt(vectors_here * vec_size)
    half = vectors_here // 2
    pair = (half + 1) // 2
    smem = pl.BlockSpec(memory_space=pltpu.SMEM)

    blank = call(
        blank_kernel,
        jax.ShapeDtypeStruct((8, 128), jnp.float32),
        [],
        vmem(1)[0],
        (),
        pl.CostEstimate(flops=10**11, bytes_accessed=256 * 2**20, transcendentals=0),
    )()
    parent = call(
        parent_kernel,
        jax.ShapeDtypeStruct((8, 128), jnp.float32),
        [smem] + vmem(1),
        vmem(1)[0],
    )(parents, blank)
    mine, part = call(
        half_kernel,
        (
            jax.ShapeDtypeStruct((half, occupied, basis), cholesky.dtype),
            jax.ShapeDtypeStruct((pair, occupied, basis), cholesky.dtype),
        ),
        vmem(2),
        vmem(2),
    )(parent, cholesky)
    far = [
        lax.ppermute(
            mine,
            ("vec", "wlk"),
            [
                ((v ^ (2 * m + 1 - k % 2)) * wlk_size + k, v * wlk_size + k)
                for v in range(vec_size)
                for k in range(wlk_size)
            ],
        )
        for m in range(1, vec_size // 2)
    ]
    near = swap(part, "vec", lambda i: i ^ 1)

    payload = call(
        payload_kernel,
        jax.ShapeDtypeStruct((occupied + EXTRA, basis), jnp.bfloat16),
        [smem] + vmem(2),
        vmem(1)[0],
    )(log_weights, parent, orbitals)
    row = lax.all_gather(payload, "wlk", axis=0)
    chosen, chosen_extra, neighbour = call(
        select_kernel,
        (
            jax.ShapeDtypeStruct((occupied, basis), jnp.bfloat16),
            jax.ShapeDtypeStruct((EXTRA, basis), jnp.bfloat16),
            jax.ShapeDtypeStruct((occupied, basis), jnp.bfloat16),
        ),
        vmem(1),
        vmem(3),
    )(row)

    *far, near, chosen = lax.optimization_barrier((*far, near, chosen))
    lacking = half - pair
    sent = lax.dynamic_slice_in_dim(near, lax.axis_index("wlk") % 2 * (pair - lacking), lacking, 0)
    vectors = [mine, near, *far]
    other = [swap(jnp.concatenate([sent, *far], axis=0), "wlk", lambda i: i ^ 1)]
    to_send = partial_gradient(norm_scale, neighbour, vectors, jnp.float32)
    to_send = partial_gradient(norm_scale, neighbour, other, jnp.bfloat16, to_send)
    received = swap(to_send, "wlk", lambda i: i ^ 3)
    own_part = partial_gradient(norm_scale, chosen, [*vectors, *other], jnp.float32)

    new_orbitals, new_logs = call(
        final_kernel,
        (
            jax.ShapeDtypeStruct((occupied, basis), jnp.float32),
            jax.ShapeDtypeStruct((1,), jnp.float32),
        ),
        vmem(5),
        [pl.BlockSpec(memory_space=pltpu.VMEM), smem],
    )(chosen, chosen_extra, own_part, received, propagator.T.astype(jnp.bfloat16))
    return new_orbitals.reshape(orbitals.shape), new_logs


def solution(mesh):
    placed = (
        P(("grp", "vec"), None, None),
        P(("grp", "vec", "wlk"), None, None),
        P(("grp", "vec", "wlk")),
        P(("grp", "vec", "wlk")),
        P("grp", None),
    )
    return jax.shard_map(
        local,
        mesh=mesh,
        in_specs=placed,
        out_specs=(P(("grp", "vec", "wlk"), None, None), P(("grp", "vec", "wlk"))),
        check_vma=False,
    )
```

```python
import functools
import math

import jax
import jax.numpy as jnp
from jax import lax
from jax.experimental import pallas as pl
from jax.experimental.pallas import tpu as pltpu
from jax.sharding import PartitionSpec as P

NS_ITERS = 2
EXTRA = 16

gradient_step = 0.25
energy_step = 0.002
epsilon = 1e-06

VMEM_LIMIT = 32 * 1024 * 1024


def call(body, out_shape, in_specs, out_specs, scratch=(), cost=None):
    return pl.pallas_call(
        body,
        out_shape=out_shape,
        in_specs=in_specs,
        out_specs=out_specs,
        scratch_shapes=list(scratch),
        cost_estimate=cost,
        compiler_params=pltpu.CompilerParams(vmem_limit_bytes=VMEM_LIMIT),
    )


def vmem(count):
    return [pl.BlockSpec(memory_space=pltpu.VMEM)] * count


def swap(array, axis, partner):
    size = lax.axis_size(axis)
    return lax.ppermute(array, axis, [(i, partner(i)) for i in range(size)])


def half_kernel(parent_ref, chol_ref, mine_ref, part_ref):
    half, _, basis = mine_ref.shape
    here = lax.axis_index("wlk")
    mine = chol_ref[pl.ds(lax.rem(here // 2, 2) * half, half)]
    mine_ref[...] = mine
    mine = mine.reshape(-1, basis)
    rows = part_ref.shape[0]
    part_ref[...] = jnp.where(lax.rem(here, 2) == 0, mine[:rows], mine[rows:])


def blank_kernel(out_ref):
    out_ref[...] = jnp.zeros(out_ref.shape, out_ref.dtype)


def parent_kernel(parent_ref, blank_ref, out_ref):
    out_ref[...] = blank_ref[...] + parent_ref[0].astype(jnp.float32)


def payload_kernel(log_ref, parent_ref, orbitals_ref, payload_ref):
    occupied, basis = orbitals_ref.shape[1:]
    payload_ref[:occupied, :] = orbitals_ref[0].astype(jnp.bfloat16)
    rows = lax.broadcasted_iota(jnp.int32, (EXTRA, basis), 0)
    value = jnp.full((EXTRA, basis), log_ref[0])
    high = value.astype(jnp.bfloat16).astype(jnp.float32)
    middle = (value - high).astype(jnp.bfloat16).astype(jnp.float32)
    low = value - high - middle
    parent = jnp.broadcast_to(parent_ref[:1, :1], value.shape)
    payload_ref[occupied:, :] = jnp.where(
        rows == 0, high, jnp.where(rows == 1, middle, jnp.where(rows == 2, low, parent))
    ).astype(jnp.bfloat16)


def select_kernel(row_ref, theta_ref, extra_ref, other_ref):
    occupied, basis = theta_ref.shape
    here = lax.axis_index("wlk")

    def chosen(target, whole):
        extra = row_ref[target, occupied:, :].astype(jnp.float32)
        place = jnp.broadcast_to(extra[3:4, :], (whole, basis))
        picked = row_ref[0, :whole].astype(jnp.float32)
        for index in range(1, row_ref.shape[0]):
            picked = jnp.where(place == index, row_ref[index, :whole].astype(jnp.float32), picked)
        return picked.astype(jnp.bfloat16)

    own = chosen(here, row_ref.shape[1])
    theta_ref[...] = own[:occupied]
    extra_ref[...] = own[occupied:]
    other_ref[...] = chosen(jnp.bitwise_xor(here, 3), occupied)


def gradient_kernel(norm_scale, blocks, exchanged, theta_ref, *refs):
    *in_refs, out_ref, adjoint = refs
    occupied, basis = theta_ref.shape
    theta = theta_ref[...]
    rows = lax.broadcasted_iota(jnp.int32, (occupied, occupied), 0)
    columns = lax.broadcasted_iota(jnp.int32, (occupied, occupied), 1)
    diagonal = rows == columns
    chols = [ref[...].reshape(-1, basis) for ref in in_refs[:blocks]]
    if exchanged:
        part_ref, other_ref = in_refs[blocks : blocks + 2]
        part, other = part_ref[...], other_ref[: part_ref.shape[0], :]
        is_first = lax.rem(lax.axis_index("wlk"), 2) == 0
        chols.append(
            jnp.concatenate(
                [jnp.where(is_first, part, other), jnp.where(is_first, other, part)], axis=0
            )
        )
        chols.append(other_ref[part_ref.shape[0] :, :])
    sum_refs = in_refs[blocks + 2 * exchanged :]
    turned = [
        lax.dot_general(chol, theta, (((1,), (1,)), ((), ())), preferred_element_type=jnp.float32)
        for chol in chols
    ]
    place = 0
    for product in turned:
        product = product.astype(jnp.bfloat16).astype(jnp.float32)
        for g in range(product.shape[0] // occupied):
            block = product[g * occupied : (g + 1) * occupied, :]
            on_diagonal = jnp.where(diagonal, block, 0.0)
            trace = jnp.sum(jnp.sum(on_diagonal, axis=0, keepdims=True), axis=1, keepdims=True)
            piece = norm_scale * (jnp.where(diagonal, trace, 0.0) - block)
            adjoint[:, place : place + occupied] = piece.astype(jnp.bfloat16)
            place += occupied
    total = sum_refs[0][...] if sum_refs else None
    place = 0
    for chol in chols:
        width = chol.shape[0]
        term = jnp.dot(
            adjoint[:, place : place + width], chol, preferred_element_type=jnp.float32
        )
        total = term if total is None else total + term
        place += width
    out_ref[...] = total.astype(out_ref.dtype)


def partial_gradient(norm_scale, theta, chols, exchanged, dtype, *summand):
    occupied, basis = theta.shape
    arrays = [*chols, *exchanged]
    width = sum(math.prod(a.shape[:-1]) for a in arrays)
    return call(
        functools.partial(gradient_kernel, norm_scale, len(chols), len(exchanged) // 2),
        jax.ShapeDtypeStruct((occupied, basis), dtype),
        vmem(1 + len(arrays) + len(summand)),
        pl.BlockSpec(memory_space=pltpu.VMEM),
        [pltpu.VMEM((occupied, width), jnp.bfloat16)],
    )(theta, *arrays, *summand)


def final_kernel(theta_ref, extra_ref, own_ref, other_ref, propagator_ref, out_ref, log_ref):
    occupied, basis = theta_ref.shape
    theta = theta_ref[...].astype(jnp.float32)
    gradient = own_ref[...] + other_ref[...].astype(jnp.float32)
    energy = 0.5 * jnp.sum(theta * gradient)
    log_weight = jnp.sum(extra_ref[...].astype(jnp.float32)[:3, :1])
    log_ref[0] = log_weight - energy_step * energy
    stepped = (theta - gradient_step * gradient).astype(jnp.bfloat16)
    propagated = jnp.dot(stepped, propagator_ref[...], preferred_element_type=jnp.float32)
    narrow = propagated.astype(jnp.bfloat16)
    overlap = lax.dot_general(
        narrow, narrow, (((1,), (1,)), ((), ())), preferred_element_type=jnp.float32
    )
    diagonal = lax.broadcasted_iota(jnp.int32, overlap.shape, 0) == lax.broadcasted_iota(
        jnp.int32, overlap.shape, 1
    )
    squares = jnp.sum(jnp.where(diagonal, overlap, 0.0), keepdims=True)
    scale = lax.rsqrt(squares / (occupied * basis) + epsilon)
    overlap = overlap * scale * (scale * (0.5 / basis))
    current = propagated * scale
    for index in range(NS_ITERS):
        if index:
            narrow = current.astype(jnp.bfloat16)
            overlap = lax.dot_general(
                narrow, narrow, (((1,), (1,)), ((), ())), preferred_element_type=jnp.float32
            ) * (0.5 / basis)
        else:
            narrow = current.astype(jnp.bfloat16)
        current = 1.5 * current - jnp.dot(
            overlap.astype(jnp.bfloat16), narrow, preferred_element_type=jnp.float32
        )
    out_ref[...] = current


def local(cholesky, orbitals, log_weights, parents, propagator):
    walker_count, occupied, basis = orbitals.shape
    vectors_here = cholesky.shape[0]
    vec_size, wlk_size = lax.axis_size("vec"), lax.axis_size("wlk")
    norm_scale = 1.0 / math.sqrt(vectors_here * vec_size)
    half = vectors_here // 2
    smem = pl.BlockSpec(memory_space=pltpu.SMEM)

    blank = call(
        blank_kernel,
        jax.ShapeDtypeStruct((8, 128), jnp.float32),
        [],
        vmem(1)[0],
        (),
        pl.CostEstimate(flops=10**11, bytes_accessed=256 * 2**20, transcendentals=0),
    )()
    parent = call(
        parent_kernel,
        jax.ShapeDtypeStruct((8, 128), jnp.float32),
        [smem] + vmem(1),
        vmem(1)[0],
    )(parents, blank)
    mine, part = call(
        half_kernel,
        (
            jax.ShapeDtypeStruct((half, occupied, basis), cholesky.dtype),
            jax.ShapeDtypeStruct((half * occupied // 2, basis), cholesky.dtype),
        ),
        vmem(2),
        vmem(2),
    )(parent, cholesky)
    far = [
        lax.ppermute(
            mine,
            ("vec", "wlk"),
            [
                ((v ^ (2 * m + 1 - k % 2)) * wlk_size + k, v * wlk_size + k)
                for v in range(vec_size)
                for k in range(wlk_size)
            ],
        )
        for m in range(1, vec_size // 2)
    ]
    near = swap(part, "vec", lambda i: i ^ 1)

    payload = call(
        payload_kernel,
        jax.ShapeDtypeStruct((occupied + EXTRA, basis), jnp.bfloat16),
        [smem] + vmem(2),
        vmem(1)[0],
    )(log_weights, parent, orbitals)
    row = lax.all_gather(payload, "wlk", axis=0)
    chosen, chosen_extra, neighbour = call(
        select_kernel,
        (
            jax.ShapeDtypeStruct((occupied, basis), jnp.bfloat16),
            jax.ShapeDtypeStruct((EXTRA, basis), jnp.bfloat16),
            jax.ShapeDtypeStruct((occupied, basis), jnp.bfloat16),
        ),
        vmem(1),
        vmem(3),
    )(row)

    *far, near, chosen = lax.optimization_barrier((*far, near, chosen))
    fetched = jnp.concatenate([near, *[c.reshape(-1, basis) for c in far]], axis=0)
    exchanged = [near, swap(fetched, "wlk", lambda i: i ^ 1)]
    vectors = [mine, *far]
    to_send = partial_gradient(norm_scale, neighbour, vectors, [], jnp.float32)
    to_send = partial_gradient(norm_scale, neighbour, [], exchanged, jnp.bfloat16, to_send)
    received = swap(to_send, "wlk", lambda i: i ^ 3)
    own_part = partial_gradient(norm_scale, chosen, vectors, exchanged, jnp.float32)

    new_orbitals, new_logs = call(
        final_kernel,
        (
            jax.ShapeDtypeStruct((occupied, basis), jnp.float32),
            jax.ShapeDtypeStruct((1,), jnp.float32),
        ),
        vmem(5),
        [pl.BlockSpec(memory_space=pltpu.VMEM), smem],
    )(chosen, chosen_extra, own_part, received, propagator.T.astype(jnp.bfloat16))
    return new_orbitals.reshape(orbitals.shape), new_logs


def solution(mesh):
    placed = (
        P(("grp", "vec"), None, None),
        P(("grp", "vec", "wlk"), None, None),
        P(("grp", "vec", "wlk")),
        P(("grp", "vec", "wlk")),
        P("grp", None),
    )
    return jax.shard_map(
        local,
        mesh=mesh,
        in_specs=placed,
        out_specs=(P(("grp", "vec", "wlk"), None, None), P(("grp", "vec", "wlk"))),
        check_vma=False,
    )
```
